32 devices in a mesh: dp: 4 (over z), expert: 2 (over y), tensor: 4 (over x, core).
Axes of the slice: x: 2, y: 2, z: 4, core: 2. Of those that a mesh axis runs over, the one named last changes fastest.
Arguments:
- tokens: bfloat16 [128, 2048], P(('dp', 'expert', 'tensor')), may hold values from -6 to 6
- routes: int32 [128, 6], P(('dp', 'expert')), may hold values from 0 to 15, as said below
- positions: int32 [128, 6], P(('dp', 'expert')), may hold values from 0 to 7, as said below
- combine_weights: float32 [128, 6], P(('dp', 'expert')), may hold values from 0.1 to 1
- cotangent: bfloat16 [128, 2048], P(('dp', 'expert', 'tensor')), may hold values from -6 to 6
- gate_weight: bfloat16 [16, 2048, 1408], P('expert', None, 'tensor'), may hold values from -0.125 to 0.125
- up_weight: bfloat16 [16, 2048, 1408], P('expert', None, 'tensor'), may hold values from -0.125 to 0.125
- down_weight: bfloat16 [16, 2048, 1408], P('expert', None, 'tensor'), may hold values from -0.15625 to 0.15625
Outputs:
- layer_out: bfloat16 [128, 2048], P(('dp', 'expert', 'tensor'))
- grad_tokens: bfloat16 [128, 2048], P(('dp', 'expert', 'tensor'))
- grad_down: bfloat16 [16, 2048, 1408], P('expert', 'dp', 'tensor')
The draws below stay inside these ranges and needn't reach their ends.
Inputs may be any that keep to these rules, and one draw needn't show every extreme that they name: `routes`: each row names 6 different experts. Within each aligned block of 16 rows, no expert is named by more than 8 rows, and one expert, the same in every block, is named by exactly 8 rows. `positions`: within each aligned block of 16 rows, no two choices share both expert and position.
All inputs are finite; a program needn't handle non-finite values.
Results may differ from the reference program's by a relative error of at most 0.017.
Values may be sent and summed in bfloat16 or wider, within the bound.
No kernel may reach another device: no remote copies, remote signals or barrier semaphores. Data moves between devices by JAX's collectives and lax.ppermute only.
A program may use at most 128 MiB of HBM per device.

```python
import math
import jax
import jax.numpy as jnp
from jax import lax

D = 2048
FF = 1408
TOP = 6
EXPERTS = 16
GROUP = 16
CAP = 8
TOKENS = 128
N_DP = 4
N_EXPERT = 2
N_TENSOR = 4


def route_plan(key):
    blocks = TOKENS // GROUP
    slot_count = EXPERTS * CAP
    extra = TOP * GROUP - CAP
    base_key = jax.random.fold_in(key, 7)
    full_expert = jax.random.randint(jax.random.fold_in(base_key, 1), (), 0, EXPERTS)

    def one_block(block_key):
        order_key, slot_key = jax.random.split(block_key)
        ranks = jax.random.permutation(order_key, EXPERTS).astype(jnp.int32)
        ranks = jnp.where(jnp.arange(EXPERTS, dtype=jnp.int32) == full_expert, -1, ranks)
        ordering = jnp.argsort(ranks).astype(jnp.int32)
        chosen_rest = jax.random.permutation(slot_key, slot_count - CAP)[:extra].astype(jnp.int32) + CAP
        chosen = jnp.sort(jnp.concatenate([jnp.arange(CAP, dtype=jnp.int32), chosen_rest]))
        layout = chosen.reshape(TOP, GROUP).T
        return (ordering[layout // CAP], layout % CAP)
    block_keys = jax.random.split(jax.random.fold_in(base_key, 2), blocks)
    experts_drawn, places_drawn = jax.vmap(one_block)(block_keys)
    return (experts_drawn.reshape(TOKENS, TOP).astype(jnp.int32), places_drawn.reshape(TOKENS, TOP).astype(jnp.int32))


def draw_routes(key, part):
    return route_plan(key)[0]


def draw_positions(key, part):
    return route_plan(key)[1]


def block_scale(key, shape, shards, low, high):
    loudness = 1.0
    for axis_at, blocks in shards:
        steps = jax.random.uniform(jax.random.fold_in(jax.random.fold_in(key, 6), axis_at), (blocks,), jnp.float32, low / len(shards), high / len(shards))
        loudness = loudness * jnp.repeat(jnp.exp(steps), shape[axis_at] // blocks).reshape((-1,) + (1,) * (len(shape) - 1 - axis_at))
    return loudness


def normal_values(own_key, shape, scale, bound, shards=(), kind=jnp.bfloat16):
    drawn = jax.random.normal(own_key, shape, jnp.float32) * scale
    if len(shards) > 0:
        drawn = block_scale(own_key, shape, shards, -0.22, 0.18) * drawn
    return jnp.clip(drawn, min=-bound, max=bound).astype(kind)


def setup_inputs(seed: int = 0) -> dict:
    keys = jax.random.split(jax.random.key(seed), 9)
    return {
        "tokens": normal_values(keys[0], (TOKENS, D), 1.0, 6.0, ((0, 32),)),
        "routes": draw_routes(jax.random.fold_in(keys[8], 71), 0),
        "positions": draw_positions(jax.random.fold_in(keys[8], 71), 0),
        "combine_weights": jnp.clip(jnp.exp(math.log(1.0) - 2.3025851 * jax.random.uniform(keys[3], (TOKENS, TOP), jnp.float32) ** block_scale(keys[3], (TOKENS, TOP), ((0, 8),), -0.2, 0.2)), 0.1, 1.0),
        "cotangent": normal_values(keys[4], (TOKENS, D), 1.0, 6.0, ((0, 32),)),
        "gate_weight": normal_values(keys[5], (EXPERTS, D, FF), D ** -0.5, 0.125, ((0, 2), (2, 4))),
        "up_weight": normal_values(keys[6], (EXPERTS, D, FF), D ** -0.5, 0.125, ((0, 2), (2, 4))),
        "down_weight": normal_values(keys[7], (EXPERTS, D, FF), FF ** -0.5, 0.15625, ((0, 2), (2, 4))),
    }


def expert_terms(carry, items):
    slot_back, activation = items
    term = jnp.einsum("erd,erf->edf", slot_back.astype(jnp.float32), activation.astype(jnp.float32), precision=lax.Precision.HIGHEST)
    return carry + lax.optimization_barrier(term.astype(jnp.bfloat16)).astype(jnp.float32), None


def reference(tokens, routes, positions, combine_weights, cotangent, gate_weight, up_weight, down_weight):
    groups = tokens.shape[0] // GROUP
    width = tokens.shape[1]
    slot_count = EXPERTS * CAP
    quarter = FF // N_TENSOR
    highest = lax.Precision.HIGHEST
    slot_index = (routes * CAP + positions).reshape(groups, GROUP, TOP)
    probs = combine_weights.reshape(groups, GROUP, TOP)
    matches = (slot_index[:, :, :, None] == jnp.arange(slot_count, dtype=jnp.int32)).astype(jnp.float32)
    placed = jnp.sum(matches, axis=2)
    weighted = jnp.sum(matches * probs[:, :, :, None], axis=2)
    slot_gain = jnp.sum(weighted, axis=1)

    def to_slots(rows):
        grouped = rows.astype(jnp.float32).reshape(groups, GROUP, width)
        return jnp.einsum("gts,gtd->gsd", placed, grouped, precision=highest)

    def by_expert(slots):
        return slots.reshape(groups, EXPERTS, CAP, -1).transpose(1, 0, 2, 3).reshape(EXPERTS, groups * CAP, -1)

    def by_group(slots):
        return slots.reshape(EXPERTS, groups, CAP, -1).transpose(1, 0, 2, 3).reshape(groups, slot_count, -1)

    def project(left, right):
        return jnp.einsum("erd,edf->erf", left.astype(jnp.float32), right.astype(jnp.float32), precision=highest)

    def by_quarter(left, right):
        left_blocks = left.astype(jnp.float32).reshape(EXPERTS, -1, N_TENSOR, quarter)
        right_blocks = right.astype(jnp.float32).reshape(EXPERTS, width, N_TENSOR, quarter)
        return jnp.einsum("erqf,edqf->qerd", left_blocks, right_blocks, precision=highest)

    def block_sum(parts):
        return jnp.sum(lax.optimization_barrier(parts.astype(jnp.bfloat16)).astype(jnp.float32), axis=0)

    dispatched = by_expert(to_slots(tokens)).astype(jnp.bfloat16)
    gate_pre = project(dispatched, gate_weight)
    up_pre = project(dispatched, up_weight)
    activation = (jax.nn.silu(gate_pre) * up_pre).astype(jnp.bfloat16)
    expert_out = by_group(block_sum(by_quarter(activation, down_weight)))
    layer_out = jnp.einsum("gts,gsd->gtd", weighted, expert_out, precision=highest)
    layer_out = layer_out.reshape(tokens.shape[0], width).astype(jnp.bfloat16)

    slot_cotangent = by_expert(to_slots(cotangent) * slot_gain[:, :, None]).astype(jnp.bfloat16)
    act_grad = jnp.einsum("erd,edf->erf", slot_cotangent.astype(jnp.float32), down_weight.astype(jnp.float32), precision=highest)
    squash = jax.nn.sigmoid(gate_pre)
    gate_back = (act_grad * up_pre * squash * (1.0 + gate_pre * (1.0 - squash))).astype(jnp.bfloat16)
    up_back = (act_grad * jax.nn.silu(gate_pre)).astype(jnp.bfloat16)
    input_part = by_quarter(gate_back, gate_weight) + by_quarter(up_back, up_weight)
    input_slots = by_group(block_sum(input_part))
    grad_tokens = jnp.einsum("gts,gsd->gtd", placed, input_slots, precision=highest)
    grad_tokens = grad_tokens.reshape(tokens.shape[0], width).astype(jnp.bfloat16)

    def split(values):
        return values.reshape(EXPERTS, N_DP, N_EXPERT * CAP, -1).transpose(1, 0, 2, 3)

    zeros = jnp.zeros((EXPERTS, width, FF), jnp.float32)
    total, unused = lax.scan(expert_terms, zeros, (split(slot_cotangent), split(activation)))
    grad_down = (total * (1.0 / N_DP)).astype(jnp.bfloat16)
    return (layer_out, grad_tokens, grad_down)
```

```python
import functools

import jax
import jax.numpy as jnp
from jax import lax
from jax.experimental import pallas as pl
from jax.experimental.pallas import tpu as pltpu
from jax.sharding import PartitionSpec as P

F32 = jnp.float32
BF16 = jnp.bfloat16
LANES = 128
NT = (((1,), (1,)), ((), ()))
TN = (((0,), (0,)), ((), ()))


def whole_part(values, divisor):
    return jnp.floor((values + 0.5) * (1.0 / divisor))


def fiota(shape, axis):
    return lax.broadcasted_iota(jnp.int32, shape, axis).astype(F32)


def slot_tables(routing, top, first_expert, capacity, groups, slots):
    rows = routing.shape[0]
    lane = fiota((rows, slots), 1)
    token = fiota((rows, slots), 0)
    expert = whole_part(lane, groups * capacity)
    inner = lane - expert * (groups * capacity)
    group = whole_part(inner, capacity)
    target = (expert + first_expert) * capacity + inner - group * capacity
    target = jnp.where(whole_part(token, rows // groups) == group, target, -1.0)
    names = routing[:, :top] * float(capacity) + routing[:, top : 2 * top]
    weights = routing[:, 2 * top : 3 * top] + routing[:, 3 * top : 4 * top]
    chosen = jnp.zeros((rows, slots), F32)
    gains = jnp.zeros((rows, slots), F32)
    for k in range(top):
        match = names[:, k : k + 1] == target
        chosen = chosen + jnp.where(match, 1.0, 0.0)
        gains = gains + jnp.where(match, weights[:, k : k + 1], 0.0)
    return chosen, gains


def column_blocks(width):
    return [(at, min(LANES, width - at)) for at in range(0, width, LANES)]


def experts_kernel(
    sizes, x_ref, gate_hbm, up_hbm, down_hbm, keep_ref, send_ref, *rest
):
    top, capacity, groups, tensor, replicas = sizes
    packs = rest[:replicas]
    gate_w, up_w, down_w, filled, results, act, sems = rest[replicas:]
    experts, hidden, width = gate_hbm.shape
    rows = x_ref.shape[0]
    slots = filled.shape[0]
    per_expert = slots // experts
    ahead = min(3, experts)

    def fetch(e):
        return [
            pltpu.make_async_copy(source.at[e], target.at[e], sems.at[e, i])
            for i, (source, target) in enumerate(
                ((gate_hbm, gate_w), (up_hbm, up_w), (down_hbm, down_w))
            )
        ]

    for e in range(ahead):
        for copy in fetch(e):
            copy.start()

    first_expert = (lax.axis_index("expert") * experts).astype(F32)
    routing = x_ref[:, 2 * width :].astype(F32)
    chosen, gains = slot_tables(routing, top, first_expert, capacity, groups, slots)
    chooser = chosen.astype(BF16)
    scatter = chosen.T.astype(BF16)
    gain = jnp.sum(gains.T, axis=1, keepdims=True)
    step = min(512, width)
    for at in range(0, width, step):
        filled[:, at : at + step] = jnp.dot(
            scatter, x_ref[:, at : at + step], preferred_element_type=F32
        ).astype(BF16)
    for at in range(width, 2 * width, step):
        filled[:, at : at + step] = (
            gain * jnp.dot(scatter, x_ref[:, at : at + step], preferred_element_type=F32)
        ).astype(BF16)

    def one_expert(e, _):
        for copy in fetch(e):
            copy.wait()

        @pl.when(e + ahead < experts)
        def _():
            for copy in fetch(e + ahead):
                copy.start()

        here = pl.ds(pl.multiple_of(e * per_expert, per_expert), per_expert)
        slot_rows = filled[here, :width]
        slot_grads = filled[here, width:]
        gate_pre = lax.dot_general(slot_rows, gate_w[e], NT, preferred_element_type=F32)
        up_pre = lax.dot_general(slot_rows, up_w[e], NT, preferred_element_type=F32)
        act_grad = lax.dot_general(slot_grads, down_w[e], NT, preferred_element_type=F32)
        squash = 1.0 / (1.0 + jnp.exp(-gate_pre))
        swish = gate_pre * squash
        activation = (swish * up_pre).astype(BF16)
        act[here, :] = activation
        gate_back = (act_grad * up_pre * squash * (1.0 + gate_pre * (1.0 - squash))).astype(BF16)
        up_back = (act_grad * swish).astype(BF16)
        results[here, :width] = jnp.dot(
            activation, down_w[e], preferred_element_type=F32
        ).astype(BF16)
        results[here, width:] = (
            jnp.dot(gate_back, gate_w[e], preferred_element_type=F32)
            + jnp.dot(up_back, up_w[e], preferred_element_type=F32)
        ).astype(BF16)
        return 0

    lax.fori_loop(0, experts, one_expert, 0)

    device = lax.axis_index("expert") * tensor + lax.axis_index("tensor")
    pair = lax.div(device, 2)
    parity = device - pair * 2
    per_device = rows // (groups * tensor)
    half = rows // 2
    row = lax.broadcasted_iota(jnp.int32, (rows, 1), 0)
    second = jnp.where(row >= half, 1, 0)
    within = row - second * half
    block = lax.div(within, jnp.full_like(within, per_device))
    token = (
        (block ^ pair) * (2 * per_device)
        + (second ^ parity) * per_device
        + within
        - block * per_device
    )
    order = jnp.where(lax.broadcasted_iota(jnp.int32, (rows, rows), 1) == token, 1.0, 0.0)
    picker = jnp.dot(order.astype(BF16), chooser, preferred_element_type=F32).astype(BF16)
    for at in range(0, 2 * width, step):
        piece = results[:, at : at + step]
        if at < width:
            piece = (piece.astype(F32) * gain).astype(BF16)
        total = jnp.dot(picker, piece, preferred_element_type=F32)
        keep_ref[:, at : at + step] = total[:half].astype(BF16)
        send_ref[:, at : at + step] = total[half:].astype(BF16)

    replica = lax.axis_index("dp")
    share = width // replicas
    for k in range(replicas):
        peer = replica ^ k
        at = 0
        for lane, size in column_blocks(hidden):
            packs[k][at : at + slots, :size] = act[:, lane : lane + size]
            if size < LANES:
                packs[k][at : at + slots, size:] = jnp.zeros((slots, LANES - size), BF16)
            at += slots
        for lane in range(0, share, LANES):
            column = pl.multiple_of(width + peer * share + lane, LANES)
            packs[k][at : at + rows, :] = x_ref[:, pl.ds(column, LANES)]
            at += rows
        packs[k][at : at + rows, :] = x_ref[:, 2 * width :]


def grad_kernel(sizes, *refs):
    top, capacity, groups, experts, hidden, rows, replicas = sizes
    packs = refs[:replicas]
    out_ref, grads, acts = refs[replicas:]
    slots = experts * groups * capacity
    per_expert = groups * capacity
    share = out_ref.shape[2]

    @pl.when(pl.program_id(0) == 0)
    def _():
        first_expert = (lax.axis_index("expert") * experts).astype(F32)
        for k in range(replicas):
            pack = packs[k]
            at = len(column_blocks(hidden)) * slots
            routing = pack[at + (share // LANES) * rows :, :].astype(F32)
            chosen, gains = slot_tables(routing, top, first_expert, capacity, groups, slots)
            scatter = chosen.T.astype(BF16)
            gain = jnp.sum(gains.T, axis=1, keepdims=True)
            for lane in range(0, share, LANES):
                grads[k, :, lane : lane + LANES] = (
                    gain * jnp.dot(scatter, pack[at : at + rows, :], preferred_element_type=F32)
                ).astype(BF16)
                at += rows
            at = 0
            for lane, size in column_blocks(hidden):
                acts[k, :, lane : lane + LANES] = pack[at : at + slots, :]
                at += slots

    e = pl.program_id(0)
    here = pl.ds(pl.multiple_of(e * per_expert, per_expert), per_expert)
    left = jnp.concatenate([acts[k, here, :] for k in range(replicas)], axis=0)
    right = jnp.concatenate([grads[k, here, :] for k in range(replicas)], axis=0)
    total = lax.dot_general(left, right, TN, preferred_element_type=F32)
    out_ref[0] = (total[:hidden] * (1.0 / replicas)).astype(BF16)


def vmem_specs(count):
    return [pl.BlockSpec(memory_space=pltpu.VMEM)] * count


def shards(
    tokens, routes, positions, combine_weights, cotangent, gate_weight, up_weight, down_weight
):
    experts, width, hidden = gate_weight.shape
    replicas = lax.axis_size("dp")
    groups = lax.axis_size("expert")
    tensor = lax.axis_size("tensor")
    group_size, top = routes.shape
    capacity = group_size // 2
    slots = experts * groups * capacity
    mine = tokens.shape[0]
    devices = groups * tensor
    rows = mine * devices
    both = ("expert", "tensor")

    first = lax.axis_index("tensor") * mine
    high = lax.reduce_precision(combine_weights, 8, 7)
    routing = jnp.concatenate(
        [routes.astype(F32), positions.astype(F32), high, combine_weights - high], axis=1
    ).astype(BF16)
    routing = lax.dynamic_slice_in_dim(routing, first, mine, axis=0)
    routing = jnp.pad(routing, ((0, 0), (0, LANES - 4 * top)))
    sent = jnp.concatenate([tokens, cotangent, routing], axis=1)
    gathered = lax.all_gather(sent, both, axis=0, tiled=True)

    pack_rows = len(column_blocks(hidden)) * slots + (width // replicas // LANES + 1) * rows
    weights = [jnp.swapaxes(w, 1, 2) for w in (gate_weight, up_weight, down_weight)]
    half = jax.ShapeDtypeStruct((rows // 2, 2 * width), BF16)
    pack = jax.ShapeDtypeStruct((pack_rows, LANES), BF16)
    outs = pl.pallas_call(
        functools.partial(experts_kernel, (top, capacity, groups, tensor, replicas)),
        out_shape=[half, half] + [pack] * replicas,
        in_specs=vmem_specs(1) + [pl.BlockSpec(memory_space=pl.ANY)] * 3,
        out_specs=vmem_specs(2 + replicas),
        scratch_shapes=[pltpu.VMEM((experts, hidden, width), BF16)] * 3
        + [
            pltpu.VMEM((slots, 2 * width), BF16),
            pltpu.VMEM((slots, 2 * width), BF16),
            pltpu.VMEM((slots, hidden), BF16),
            pltpu.SemaphoreType.DMA((experts, 3)),
        ],
        compiler_params=pltpu.CompilerParams(vmem_limit_bytes=48 * 2**20),
        cost_estimate=pl.CostEstimate(
            flops=12 * slots * hidden * width,
            bytes_accessed=6 * experts * hidden * width,
            transcendentals=slots * hidden,
        ),
        name="experts",
    )(gathered, *weights)
    keep, send, packs = outs[0], outs[1], outs[2:]

    def swap(values, distance):
        return lax.ppermute(values, both, [(i, i ^ distance) for i in range(devices)])

    near = keep.astype(F32) + swap(send, 1).astype(F32)
    near = near.reshape(devices // 2, mine, 2 * width)
    total = near[0]
    for k in range(1, devices // 2):
        total = total + swap(near[k].astype(BF16), 2 * k).astype(F32)
    total = total.astype(BF16)

    arrived = [packs[0]]
    for k in range(1, replicas):
        arrived.append(lax.ppermute(packs[k], "dp", [(i, i ^ k) for i in range(replicas)]))
    share = width // replicas
    grad = pl.pallas_call(
        functools.partial(
            grad_kernel, (top, capacity, groups, experts, hidden, rows, replicas)
        ),
        grid=(experts,),
        out_shape=jax.ShapeDtypeStruct((experts, hidden, share), BF16),
        in_specs=vmem_specs(replicas),
        out_specs=pl.BlockSpec((1, hidden, share), lambda e: (e, 0, 0)),
        scratch_shapes=[
            pltpu.VMEM((replicas, slots, share), BF16),
            pltpu.VMEM((replicas, slots, len(column_blocks(hidden)) * LANES), BF16),
        ],
        compiler_params=pltpu.CompilerParams(vmem_limit_bytes=24 * 2**20),
        cost_estimate=pl.CostEstimate(
            flops=2 * replicas * slots * share * hidden,
            bytes_accessed=2 * experts * share * hidden,
            transcendentals=0,
        ),
        name="grad_down",
    )(*arrived)
    return (total[:, :width], total[:, width:], jnp.swapaxes(grad, 1, 2))


def solution(mesh):
    return jax.shard_map(
        shards,
        mesh=mesh,
        in_specs=(
            P(("dp", "expert", "tensor"), None),
            P(("dp", "expert"), None),
            P(("dp", "expert"), None),
            P(("dp", "expert"), None),
            P(("dp", "expert", "tensor"), None),
            P("expert", None, "tensor"),
            P("expert", None, "tensor"),
            P("expert", None, "tensor"),
        ),
        out_specs=(
            P(("dp", "expert", "tensor"), None),
            P(("dp", "expert", "tensor"), None),
            P("expert", "dp", "tensor"),
        ),
        check_vma=False,
    )
```

```python
import functools

import jax
import jax.numpy as jnp
from jax import lax
from jax.experimental import pallas as pl
from jax.experimental.pallas import tpu as pltpu
from jax.sharding import PartitionSpec as P

F32 = jnp.float32
BF16 = jnp.bfloat16
LANES = 128
NT = (((1,), (1,)), ((), ()))
TN = (((0,), (0,)), ((), ()))


def whole_part(values, divisor):
    return jnp.floor((values + 0.5) * (1.0 / divisor))


def fiota(shape, axis):
    return lax.broadcasted_iota(jnp.int32, shape, axis).astype(F32)


def slot_tables(routing, top, first_expert, capacity, groups, slots):
    rows = routing.shape[0]
    lane = fiota((rows, slots), 1)
    token = fiota((rows, slots), 0)
    expert = whole_part(lane, groups * capacity)
    inner = lane - expert * (groups * capacity)
    group = whole_part(inner, capacity)
    target = (expert + first_expert) * capacity + inner - group * capacity
    target = jnp.where(whole_part(token, rows // groups) == group, target, -1.0)
    names = routing[:, :top] * float(capacity) + routing[:, top : 2 * top]
    weights = routing[:, 2 * top : 3 * top] + routing[:, 3 * top : 4 * top]
    chosen = jnp.zeros((rows, slots), F32)
    gains = jnp.zeros((rows, slots), F32)
    for k in range(top):
        match = names[:, k : k + 1] == target
        chosen = chosen + jnp.where(match, 1.0, 0.0)
        gains = gains + jnp.where(match, weights[:, k : k + 1], 0.0)
    return chosen, gains


def column_blocks(width):
    return [(at, min(LANES, width - at)) for at in range(0, width, LANES)]


def pack_kernel(tokens_ref, cotangent_ref, routes_ref, positions_ref, weights_ref, out_ref):
    mine, width = tokens_ref.shape
    top, group_size = routes_ref.shape
    weights = weights_ref[...]
    high = weights.astype(BF16)
    low = (weights - high.astype(F32)).astype(BF16)
    table = jnp.concatenate(
        [routes_ref[...].astype(F32), positions_ref[...].astype(F32), high.astype(F32), low.astype(F32)],
        axis=0,
    ).astype(BF16)
    first = lax.axis_index("tensor") * mine
    column = lax.broadcasted_iota(jnp.int32, (mine, group_size), 1)
    row = lax.broadcasted_iota(jnp.int32, (mine, group_size), 0)
    pick = jnp.where(column == row + first, 1.0, 0.0).astype(BF16)
    routing = lax.dot_general(pick, table, NT, preferred_element_type=F32)
    out_ref[:, :width] = tokens_ref[...]
    out_ref[:, width : 2 * width] = cotangent_ref[...]
    out_ref[:, 2 * width :] = jnp.concatenate(
        [routing, jnp.zeros((mine, LANES - 4 * top), F32)], axis=1
    ).astype(BF16)


def activations_kernel(
    sizes, x_ref, gate_hbm, up_hbm, down_hbm, gate_w, up_w, down_w, backs, picker_ref, gain_ref, *rest
):
    top, capacity, groups, tensor, replicas = sizes
    packs = rest[:replicas]
    filled, sems = rest[replicas:]
    experts, hidden, width = gate_hbm.shape
    rows = x_ref.shape[0]
    slots = filled.shape[0]
    per_expert = slots // experts
    ahead = min(3, experts)

    def fetch(e):
        return [
            pltpu.make_async_copy(source.at[e], target.at[e], sems.at[e, i])
            for i, (source, target) in enumerate(
                ((gate_hbm, gate_w), (up_hbm, up_w), (down_hbm, down_w))
            )
        ]

    for e in range(ahead):
        for copy in fetch(e):
            copy.start()

    first_expert = (lax.axis_index("expert") * experts).astype(F32)
    routing = x_ref[:, 2 * width :].astype(F32)
    chosen, gains = slot_tables(routing, top, first_expert, capacity, groups, slots)
    scatter = chosen.T.astype(BF16)
    gain = jnp.sum(gains.T, axis=1, keepdims=True)
    gain_ref[...] = gain
    step = min(512, width)
    for at in range(0, width, step):
        filled[:, at : at + step] = jnp.dot(
            scatter, x_ref[:, at : at + step], preferred_element_type=F32
        ).astype(BF16)
    for at in range(width, 2 * width, step):
        filled[:, at : at + step] = (
            gain * jnp.dot(scatter, x_ref[:, at : at + step], preferred_element_type=F32)
        ).astype(BF16)

    device = lax.axis_index("expert") * tensor + lax.axis_index("tensor")
    pair = lax.div(device, 2)
    parity = device - pair * 2
    per_device = rows // (groups * tensor)
    half = rows // 2
    row = lax.broadcasted_iota(jnp.int32, (rows, 1), 0)
    second = jnp.where(row >= half, 1, 0)
    within = row - second * half
    block = lax.div(within, jnp.full_like(within, per_device))
    token = (
        (block ^ pair) * (2 * per_device)
        + (second ^ parity) * per_device
        + within
        - block * per_device
    )
    order = jnp.where(lax.broadcasted_iota(jnp.int32, (rows, rows), 1) == token, 1.0, 0.0)
    picker_ref[...] = jnp.dot(
        order.astype(BF16), chosen.astype(BF16), preferred_element_type=F32
    ).astype(BF16)

    def one_expert(e, _):
        for copy in fetch(e):
            copy.wait()

        @pl.when(e + ahead < experts)
        def _():
            for copy in fetch(e + ahead):
                copy.start()

        here = pl.ds(pl.multiple_of(e * per_expert, per_expert), per_expert)
        slot_rows = filled[here, :width]
        slot_grads = filled[here, width:]
        gate_pre = lax.dot_general(slot_rows, gate_w[e], NT, preferred_element_type=F32)
        up_pre = lax.dot_general(slot_rows, up_w[e], NT, preferred_element_type=F32)
        act_grad = lax.dot_general(slot_grads, down_w[e], NT, preferred_element_type=F32)
        squash = 1.0 / (1.0 + jnp.exp(-gate_pre))
        swish = gate_pre * squash
        backs[0, here, :] = (swish * up_pre).astype(BF16)
        backs[1, here, :] = (
            act_grad * up_pre * squash * (1.0 + gate_pre * (1.0 - squash))
        ).astype(BF16)
        backs[2, here, :] = (act_grad * swish).astype(BF16)
        return 0

    lax.fori_loop(0, experts, one_expert, 0)

    replica = lax.axis_index("dp")
    share = width // replicas
    turned = {
        (block, lane): backs[0, block : block + LANES, lane : lane + size].T
        for block in range(0, slots, LANES)
        for lane, size in column_blocks(hidden)
    }
    for k in range(replicas):
        peer = replica ^ k
        at = 0
        for block in range(0, slots, LANES):
            for lane, size in column_blocks(hidden):
                packs[k][at : at + size, :] = turned[block, lane]
                at += size
        for lane in range(0, share, LANES):
            column = pl.multiple_of(width + peer * share + lane, LANES)
            packs[k][at : at + rows, :] = x_ref[:, pl.ds(column, LANES)]
            at += rows
        packs[k][at : at + rows, :] = x_ref[:, 2 * width :]


def outputs_kernel(
    backs, picker_ref, gain_ref, gate_w, up_w, down_w, keep_ref, send_one, send_two, results
):
    experts, _, width = gate_w.shape
    half = keep_ref.shape[0]
    slots = backs.shape[1]
    per_expert = slots // experts

    def one_expert(e, _):
        here = pl.ds(pl.multiple_of(e * per_expert, per_expert), per_expert)
        forward = jnp.dot(backs[0, here, :], down_w[e], preferred_element_type=F32)
        results[here, :width] = (forward.astype(BF16).astype(F32) * gain_ref[here, :]).astype(BF16)
        results[here, width:] = (
            jnp.dot(backs[1, here, :], gate_w[e], preferred_element_type=F32)
            + jnp.dot(backs[2, here, :], up_w[e], preferred_element_type=F32)
        ).astype(BF16)
        return 0

    lax.fori_loop(0, experts, one_expert, 0)
    step = min(512, width)
    for at in range(0, 2 * width, step):
        total = jnp.dot(picker_ref[...], results[:, at : at + step], preferred_element_type=F32)
        keep_ref[:, at : at + step] = total[:half].astype(BF16)
        send_ref = send_one if at < width else send_two
        to = at % width
        send_ref[:, to : to + step] = total[half:].astype(BF16)


def grad_kernel(sizes, *refs):
    top, capacity, groups, replicas = sizes
    packs = refs[:replicas]
    own_ref, out_hbm, own_out, grads, acts, result, sems = refs[replicas:]
    experts, hidden, share = out_hbm.shape
    per_replica = groups * capacity
    slots = experts * per_replica
    per_expert = replicas * per_replica
    act_rows = slots // LANES * hidden
    rows = (packs[0].shape[0] - act_rows) // (share // LANES + 1)

    first_expert = (lax.axis_index("expert") * experts).astype(F32)
    for k in range(replicas):
        at = act_rows
        routing = packs[k][at + (share // LANES) * rows :, :].astype(F32)
        chosen, gains = slot_tables(routing, top, first_expert, capacity, groups, slots)
        scatter = chosen.T.astype(BF16)
        gain = jnp.sum(gains.T, axis=1, keepdims=True)
        for lane in range(0, share, LANES):
            filled = jnp.dot(scatter, packs[k][at : at + rows, :], preferred_element_type=F32)
            filled = (gain * filled).astype(BF16)
            for e in range(experts):
                to = e * per_expert + k * per_replica
                grads[to : to + per_replica, lane : lane + LANES] = filled[
                    e * per_replica : (e + 1) * per_replica
                ]
            at += rows

    left = jnp.concatenate(
        [
            packs[k][block * hidden : (block + 1) * hidden, :]
            for k in range(replicas)
            for block in range(slots // LANES)
        ],
        axis=1,
    )
    if experts > 1:
        lanes = replicas * slots
        before = fiota((lanes, lanes), 0)
        after = fiota((lanes, lanes), 1)
        source = whole_part(before, slots)
        inner = before - source * slots
        expert = whole_part(inner, per_replica)
        place = expert * per_expert + source * per_replica + inner - expert * per_replica
        order = jnp.where(place == after, 1.0, 0.0).astype(BF16)
        left = jnp.dot(left, order, preferred_element_type=F32).astype(BF16)
    acts[...] = left

    own_out[...] = own_ref[...].astype(F32)

    copies = []
    for e in range(experts):
        low = e * per_expert // LANES * LANES
        high = -(-(e + 1) * per_expert // LANES) * LANES
        right = grads[low:high, :]
        if high - low > per_expert:
            row = lax.broadcasted_iota(jnp.int32, right.shape, 0) + low
            inside = (row >= e * per_expert) & (row < (e + 1) * per_expert)
            right = jnp.where(inside, right.astype(F32), 0.0).astype(BF16)
        total = jnp.dot(acts[:, low:high], right, preferred_element_type=F32)
        result[e] = (total * (1.0 / replicas)).astype(BF16)
        copies.append(pltpu.make_async_copy(result.at[e], out_hbm.at[e], sems.at[e]))
        copies[-1].start()
    for copy in copies:
        copy.wait()


def near_kernel(mine, keep_ref, one_ref, two_ref, own_ref, *parts):
    width = one_ref.shape[1]
    for k, part in enumerate((own_ref, *parts)):
        here = slice(k * mine, (k + 1) * mine)
        for side, ref in enumerate((one_ref, two_ref)):
            columns = slice(side * width, (side + 1) * width)
            part[:, columns] = (
                keep_ref[here, columns].astype(F32) + ref[here, :].astype(F32)
            ).astype(part.dtype)


def vmem_specs(count):
    return [pl.BlockSpec(memory_space=pltpu.VMEM)] * count


def shards(
    tokens, routes, positions, combine_weights, cotangent, gate_weight, up_weight, down_weight
):
    experts, width, hidden = gate_weight.shape
    replicas = lax.axis_size("dp")
    groups = lax.axis_size("expert")
    tensor = lax.axis_size("tensor")
    group_size, top = routes.shape
    capacity = group_size // 2
    slots = experts * groups * capacity
    mine = tokens.shape[0]
    devices = groups * tensor
    rows = mine * devices
    both = ("expert", "tensor")

    sent = pl.pallas_call(
        pack_kernel,
        out_shape=jax.ShapeDtypeStruct((mine, 2 * width + LANES), BF16),
        in_specs=vmem_specs(5),
        out_specs=vmem_specs(1)[0],
        name="pack",
    )(tokens, cotangent, routes.T, positions.T, combine_weights.T)
    gathered = lax.all_gather(sent, both, axis=0, tiled=True)

    pack_rows = slots // LANES * hidden + (width // replicas // LANES + 1) * rows
    weights = [
        pltpu.with_memory_space_constraint(jnp.swapaxes(w, 1, 2), pltpu.HBM)
        for w in (gate_weight, up_weight, down_weight)
    ]
    half = jax.ShapeDtypeStruct((rows // 2, 2 * width), BF16)
    pack = jax.ShapeDtypeStruct((pack_rows, LANES), BF16)
    held = pltpu.VMEM((experts, hidden, width), BF16)
    outs = pl.pallas_call(
        functools.partial(activations_kernel, (top, capacity, groups, tensor, replicas)),
        out_shape=[held] * 3
        + [
            jax.ShapeDtypeStruct((3, slots, hidden), BF16),
            jax.ShapeDtypeStruct((rows, slots), BF16),
            jax.ShapeDtypeStruct((slots, 1), F32),
        ]
        + [pack] * replicas,
        in_specs=vmem_specs(1) + [pl.BlockSpec(memory_space=pltpu.HBM)] * 3,
        out_specs=vmem_specs(6 + replicas),
        scratch_shapes=[
            pltpu.VMEM((slots, 2 * width), BF16),
            pltpu.SemaphoreType.DMA((experts, 3)),
        ],
        compiler_params=pltpu.CompilerParams(vmem_limit_bytes=6 * 2**20),
        cost_estimate=pl.CostEstimate(
            flops=6 * slots * hidden * width,
            bytes_accessed=6 * experts * hidden * width,
            transcendentals=slots * hidden,
        ),
        name="activations",
    )(gathered, *weights)
    held_weights = [pltpu.with_memory_space_constraint(w, pltpu.VMEM) for w in outs[:3]]
    packs = outs[6:]
    side = jax.ShapeDtypeStruct((rows // 2, width), BF16)
    keep, send_one, send_two = pl.pallas_call(
        outputs_kernel,
        out_shape=[half, side, side],
        in_specs=vmem_specs(6),
        out_specs=vmem_specs(3),
        scratch_shapes=[pltpu.VMEM((slots, 2 * width), BF16)],
        compiler_params=pltpu.CompilerParams(vmem_limit_bytes=6 * 2**20),
        cost_estimate=pl.CostEstimate(
            flops=6 * slots * hidden * width,
            bytes_accessed=6 * experts * hidden * width,
            transcendentals=0,
        ),
        name="outputs",
    )(*outs[3:6], *held_weights)

    def swap(values, distance):
        return lax.ppermute(values, both, [(i, i ^ distance) for i in range(devices)])

    own, *others_near = pl.pallas_call(
        functools.partial(near_kernel, mine),
        out_shape=[jax.ShapeDtypeStruct((mine, 2 * width), F32)]
        + [jax.ShapeDtypeStruct((mine, 2 * width), BF16)] * (devices // 2 - 1),
        in_specs=vmem_specs(3),
        out_specs=vmem_specs(devices // 2),
        compiler_params=pltpu.CompilerParams(vmem_limit_bytes=2 * 2**20),
        name="near",
    )(keep, swap(send_one, 1), swap(send_two, 1))
    received = [swap(part, 2 * k) for k, part in enumerate(others_near, 1)]

    arrived = [packs[0]]
    for k in range(1, replicas):
        arrived.append(lax.ppermute(packs[k], "dp", [(i, i ^ k) for i in range(replicas)]))
    share = width // replicas
    grad, total = pl.pallas_call(
        functools.partial(grad_kernel, (top, capacity, groups, replicas)),
        out_shape=[
            jax.ShapeDtypeStruct((experts, hidden, share), BF16),
            jax.ShapeDtypeStruct((mine, 2 * width), F32),
        ],
        in_specs=vmem_specs(replicas + 1),
        out_specs=[pl.BlockSpec(memory_space=pl.ANY)] + vmem_specs(1),
        scratch_shapes=[
            pltpu.VMEM((replicas * slots, share), BF16),
            pltpu.VMEM((hidden, replicas * slots), BF16),
            pltpu.VMEM((experts, hidden, share), BF16),
            pltpu.SemaphoreType.DMA((experts,)),
        ],
        compiler_params=pltpu.CompilerParams(vmem_limit_bytes=10 * 2**20),
        cost_estimate=pl.CostEstimate(
            flops=2 * replicas * slots * share * hidden,
            bytes_accessed=2 * experts * share * hidden,
            transcendentals=0,
        ),
        name="grad_down",
    )(*arrived, own)
    for part in received:
        total = total + part.astype(F32)
    total = total.astype(BF16)
    return (total[:, :width], total[:, width:], jnp.swapaxes(grad, 1, 2))


def solution(mesh):
    return jax.shard_map(
        shards,
        mesh=mesh,
        in_specs=(
            P(("dp", "expert", "tensor"), None),
            P(("dp", "expert"), None),
            P(("dp", "expert"), None),
            P(("dp", "expert"), None),
            P(("dp", "expert", "tensor"), None),
            P("expert", None, "tensor"),
            P("expert", None, "tensor"),
            P("expert", None, "tensor"),
        ),
        out_specs=(
            P(("dp", "expert", "tensor"), None),
            P(("dp", "expert", "tensor"), None),
            P("expert", "dp", "tensor"),
        ),
        check_vma=False,
    )
```

```python
import functools

import jax
import jax.numpy as jnp
from jax import lax
from jax.experimental import pallas as pl
from jax.experimental.pallas import tpu as pltpu
from jax.sharding import PartitionSpec as P

F32 = jnp.float32
BF16 = jnp.bfloat16
LANES = 128
EARLY = 3
LEAD = 4
NT = (((1,), (1,)), ((), ()))
TN = (((0,), (0,)), ((), ()))


def whole_part(values, divisor):
    return jnp.floor((values + 0.5) * (1.0 / divisor))


def fiota(shape, axis):
    return lax.broadcasted_iota(jnp.int32, shape, axis).astype(F32)


def row_tokens(rows, devices, tensor):
    device = lax.axis_index("expert") * tensor + lax.axis_index("tensor")
    pair = lax.div(device, 2)
    parity = device - pair * 2
    mine = rows // devices
    row = lax.broadcasted_iota(jnp.int32, (rows, 1), 0)
    second = jnp.where(row >= rows // 2, 1, 0)
    within = row - second * (rows // 2)
    block = lax.div(within, jnp.full_like(within, mine))
    token = (block ^ pair) * (2 * mine) + (second ^ parity) * mine + within - block * mine
    return token.astype(F32)


def slot_tables(routing, token, top, first_expert, capacity, groups, slots):
    rows = routing.shape[0]
    lane = fiota((rows, slots), 1)
    expert = whole_part(lane, groups * capacity)
    inner = lane - expert * (groups * capacity)
    group = whole_part(inner, capacity)
    target = (expert + first_expert) * capacity + inner - group * capacity
    target = jnp.where(whole_part(token, rows // groups) == group, target, -1.0)
    names = routing[:, :top] * float(capacity) + routing[:, top : 2 * top]
    weights = routing[:, 2 * top : 3 * top] + routing[:, 3 * top : 4 * top]
    chosen = jnp.zeros((rows, slots), F32)
    gains = jnp.zeros((rows, slots), F32)
    for k in range(top):
        match = names[:, k : k + 1] == target
        chosen = chosen + jnp.where(match, 1.0, 0.0)
        gains = gains + jnp.where(match, weights[:, k : k + 1], 0.0)
    return chosen, gains


def column_blocks(width):
    return [(at, min(LANES, width - at)) for at in range(0, width, LANES)]


def fetch_experts(weights, held, sems, first, last):
    return [
        pltpu.make_async_copy(source.at[e], target.at[e], sems.at[e, i])
        for e in range(first, last)
        for i, (source, target) in enumerate(zip(weights, held))
    ]


def pack_kernel(*refs):
    sources, out_ref = refs[:5], refs[5]
    routes_ref, positions_ref, weights_ref, sems = refs[6:]
    mine, width = sources[0].shape
    top, group_size = routes_ref.shape
    targets = (
        out_ref.at[:, :width],
        out_ref.at[:, width : 2 * width],
        routes_ref,
        positions_ref,
        weights_ref,
    )
    copies = [
        pltpu.make_async_copy(source, target, sems.at[i])
        for i, (source, target) in enumerate(zip(sources, targets))
    ]
    for copy in copies:
        copy.start()
    for copy in copies:
        copy.wait()
    weights = weights_ref[...]
    high = weights.astype(BF16)
    low = (weights - high.astype(F32)).astype(BF16)
    table = jnp.concatenate(
        [routes_ref[...].astype(F32), positions_ref[...].astype(F32), high.astype(F32), low.astype(F32)],
        axis=0,
    ).astype(BF16)
    first = lax.axis_index("tensor") * mine
    column = lax.broadcasted_iota(jnp.int32, (mine, group_size), 1)
    row = lax.broadcasted_iota(jnp.int32, (mine, group_size), 0)
    pick = jnp.where(column == row + first, 1.0, 0.0).astype(BF16)
    routing = lax.dot_general(pick, table, NT, preferred_element_type=F32)
    out_ref[:, 2 * width :] = jnp.concatenate(
        [routing, jnp.zeros((mine, LANES - 4 * top), F32)], axis=1
    ).astype(BF16)


def join_kernel(*refs):
    out_ref = refs[-3]
    mine = refs[0].shape[0]
    for k, block in enumerate(refs[:-5]):
        out_ref[k * mine : (k + 1) * mine, :] = block[...]


def fetch_kernel(last, *refs):
    weights, held, sems = refs[:2], refs[2:4], refs[4]
    copies = fetch_experts(weights, held, sems, 0, last)
    for copy in copies:
        copy.start()
    for copy in copies:
        copy.wait()


def activations_kernel(
    sizes, ready, lead, x_ref, far_ref, gate_hbm, up_hbm, down_hbm, *rest
):
    top, capacity, groups, tensor, replicas = sizes
    gate_w, up_w, down_w, activations, slope_ref, swish_ref, grads_ref, picker_ref, gain_ref = rest[2:11]
    packs = rest[11 : 11 + replicas]
    filled, sems, down_sems = rest[11 + replicas :]
    experts, hidden, width = gate_hbm.shape
    half = x_ref.shape[0]
    rows = 2 * half
    slots = filled.shape[0]
    per_expert = slots // experts
    batches = [
        fetch_experts((gate_hbm, up_hbm), (gate_w, up_w), sems, first, min(first + 2, experts))
        for first in range(ready, experts, 2)
    ]
    downs = fetch_experts((down_hbm,), (down_w,), down_sems, 0, lead)
    for copy in sum(batches[:2], []):
        copy.start()

    first_expert = (lax.axis_index("expert") * experts).astype(F32)
    routing = jnp.concatenate([x_ref[:, 2 * width :], far_ref[:, 2 * width :]], axis=0).astype(F32)
    token = row_tokens(rows, groups * tensor, tensor)
    chosen, gains = slot_tables(routing, token, top, first_expert, capacity, groups, slots)
    scatter = chosen.T.astype(BF16)
    gain = jnp.sum(gains.T, axis=1, keepdims=True)
    gain_ref[...] = gain
    picker_ref[...] = chosen.astype(BF16)
    step = min(512, width)
    for at in range(0, 2 * width, step):
        given = jnp.concatenate([x_ref[:, at : at + step], far_ref[:, at : at + step]], axis=0)
        slot_rows = jnp.dot(scatter, given, preferred_element_type=F32)
        if at < width:
            filled[:, at : at + step] = slot_rows.astype(BF16)
        else:
            grads_ref[:, at - width : at - width + step] = (gain * slot_rows).astype(BF16)

    for e in range(experts):
        if e >= ready and (e - ready) % 2 == 0:
            at = (e - ready) // 2
            for copy in batches[at]:
                copy.wait()
            for copy in batches[at + 2] if at + 2 < len(batches) else []:
                copy.start()
            if at + 3 == len(batches):
                for copy in downs:
                    copy.start()
        here = slice(e * per_expert, (e + 1) * per_expert)
        slot_rows = filled[here, :]
        gate_pre = lax.dot_general(slot_rows, gate_w[e], NT, preferred_element_type=F32)
        up_pre = lax.dot_general(slot_rows, up_w[e], NT, preferred_element_type=F32)
        squash = 1.0 / (1.0 + jnp.exp(-gate_pre))
        swish = gate_pre * squash
        activations[here, :] = (swish * up_pre).astype(BF16)
        slope_ref[here, :] = up_pre * squash * (1.0 + gate_pre * (1.0 - squash))
        swish_ref[here, :] = swish
    if len(batches) < 3:
        for copy in downs:
            copy.start()

    replica = lax.axis_index("dp")
    share = width // replicas
    turned = {
        (block, lane): activations[block : block + LANES, lane : lane + size].T
        for block in range(0, slots, LANES)
        for lane, size in column_blocks(hidden)
    }
    for k in range(replicas):
        peer = replica ^ k
        at = 0
        for block in range(0, slots, LANES):
            for lane, size in column_blocks(hidden):
                packs[k][at : at + size, :] = turned[block, lane]
                at += size
        for lane in range(0, share, LANES):
            column = pl.multiple_of(width + peer * share + lane, LANES)
            packs[k][at : at + half, :] = x_ref[:, pl.ds(column, LANES)]
            packs[k][at + half : at + rows, :] = far_ref[:, pl.ds(column, LANES)]
            at += rows
        packs[k][at : at + half, :] = x_ref[:, 2 * width :]
        packs[k][at + half : at + rows, :] = far_ref[:, 2 * width :]
    for copy in downs:
        copy.wait()


def outputs_kernel(
    lead, activations, slope_ref, swish_ref, grads_ref, picker_ref, gain_ref, gate_w, up_w, unused, down_hbm,
    keep_ref, send_one, send_two, down_w, results, backs, sems
):
    experts, _, width = gate_w.shape
    half = keep_ref.shape[0]
    slots = activations.shape[0]
    per_expert = slots // experts
    copies = fetch_experts((down_hbm,), (down_w,), sems, lead, experts)
    for copy in copies:
        copy.start()
    for e in range(experts):
        if e >= lead and (e - lead) % 2 == 0:
            for copy in copies[e - lead : e - lead + 2]:
                copy.wait()
        here = slice(e * per_expert, (e + 1) * per_expert)
        act_grad = lax.dot_general(grads_ref[here, :], down_w[e], NT, preferred_element_type=F32)
        backs[0, here, :] = (act_grad * slope_ref[here, :]).astype(BF16)
        backs[1, here, :] = (act_grad * swish_ref[here, :]).astype(BF16)
        forward = jnp.dot(activations[here, :], down_w[e], preferred_element_type=F32)
        results[here, :width] = (forward.astype(BF16).astype(F32) * gain_ref[here, :]).astype(BF16)
    for e in range(experts):
        here = slice(e * per_expert, (e + 1) * per_expert)
        results[here, width:] = (
            jnp.dot(backs[0, here, :], gate_w[e], preferred_element_type=F32)
            + jnp.dot(backs[1, here, :], up_w[e], preferred_element_type=F32)
        ).astype(BF16)

    step = min(512, width)
    for at in range(0, 2 * width, step):
        total = jnp.dot(picker_ref[...], results[:, at : at + step], preferred_element_type=F32)
        keep_ref[:, at : at + step] = total[:half].astype(BF16)
        send_ref = send_one if at < width else send_two
        to = at % width
        send_ref[:, to : to + step] = total[half:].astype(BF16)


def grad_kernel(sizes, *refs):
    top, capacity, groups, tensor, replicas = sizes
    packs = refs[:replicas]
    own_ref, out_hbm, own_out, grads, acts, result, sems = refs[replicas:]
    experts, hidden, share = out_hbm.shape
    per_replica = groups * capacity
    slots = experts * per_replica
    per_expert = replicas * per_replica
    act_rows = slots // LANES * hidden
    rows = (packs[0].shape[0] - act_rows) // (share // LANES + 1)

    first_expert = (lax.axis_index("expert") * experts).astype(F32)
    token = row_tokens(rows, groups * tensor, tensor)
    for k in range(replicas):
        at = act_rows
        routing = packs[k][at + (share // LANES) * rows :, :].astype(F32)
        chosen, gains = slot_tables(
            routing, token, top, first_expert, capacity, groups, slots
        )
        scatter = chosen.T.astype(BF16)
        gain = jnp.sum(gains.T, axis=1, keepdims=True)
        for lane in range(0, share, LANES):
            filled = jnp.dot(scatter, packs[k][at : at + rows, :], preferred_element_type=F32)
            filled = (gain * filled).astype(BF16)
            for e in range(experts):
                to = e * per_expert + k * per_replica
                grads[to : to + per_replica, lane : lane + LANES] = filled[
                    e * per_replica : (e + 1) * per_replica
                ]
            at += rows

    left = jnp.concatenate(
        [
            packs[k][block * hidden : (block + 1) * hidden, :]
            for k in range(replicas)
            for block in range(slots // LANES)
        ],
        axis=1,
    )
    if experts > 1:
        lanes = replicas * slots
        before = fiota((lanes, lanes), 0)
        after = fiota((lanes, lanes), 1)
        source = whole_part(before, slots)
        inner = before - source * slots
        expert = whole_part(inner, per_replica)
        place = expert * per_expert + source * per_replica + inner - expert * per_replica
        order = jnp.where(place == after, 1.0, 0.0).astype(BF16)
        left = jnp.dot(left, order, preferred_element_type=F32).astype(BF16)
    acts[...] = left

    own_out[...] = own_ref[...].astype(F32)

    copies = []
    for e in range(experts):
        low = e * per_expert // LANES * LANES
        high = -(-(e + 1) * per_expert // LANES) * LANES
        right = grads[low:high, :]
        if high - low > per_expert:
            row = lax.broadcasted_iota(jnp.int32, right.shape, 0) + low
            inside = (row >= e * per_expert) & (row < (e + 1) * per_expert)
            right = jnp.where(inside, right.astype(F32), 0.0).astype(BF16)
        total = jnp.dot(acts[:, low:high], right, preferred_element_type=F32)
        result[e] = (total * (1.0 / replicas)).astype(BF16)
        copies.append(pltpu.make_async_copy(result.at[e], out_hbm.at[e], sems.at[e]))
        copies[-1].start()
    for copy in copies:
        copy.wait()


def near_kernel(mine, keep_ref, one_ref, two_ref, own_ref, *parts):
    width = one_ref.shape[1]
    for k, part in enumerate((own_ref, *parts)):
        here = slice(k * mine, (k + 1) * mine)
        for side, ref in enumerate((one_ref, two_ref)):
            columns = slice(side * width, (side + 1) * width)
            part[:, columns] = (
                keep_ref[here, columns].astype(F32) + ref[here, :].astype(F32)
            ).astype(part.dtype)


def hbm_specs(count):
    return [pl.BlockSpec(memory_space=pltpu.HBM)] * count


def vmem_specs(count):
    return [pl.BlockSpec(memory_space=pltpu.VMEM)] * count


def shards(
    tokens, routes, positions, combine_weights, cotangent, gate_weight, up_weight, down_weight
):
    experts, width, hidden = gate_weight.shape
    replicas = lax.axis_size("dp")
    groups = lax.axis_size("expert")
    tensor = lax.axis_size("tensor")
    group_size, top = routes.shape
    capacity = group_size // 2
    slots = experts * groups * capacity
    mine = tokens.shape[0]
    devices = groups * tensor
    rows = mine * devices
    both = ("expert", "tensor")

    def swap(values, distance):
        return lax.ppermute(values, both, [(i, i ^ distance) for i in range(devices)])

    weights = [
        pltpu.with_memory_space_constraint(jnp.swapaxes(w, 1, 2), pltpu.HBM)
        for w in (gate_weight, up_weight, down_weight)
    ]
    held = pltpu.VMEM((experts, hidden, width), BF16)
    ready = min(EARLY, experts)
    inputs = [
        pltpu.with_memory_space_constraint(x, pltpu.HBM)
        for x in (tokens, cotangent, routes.T, positions.T, combine_weights.T)
    ]
    row = jax.ShapeDtypeStruct((mine, 2 * width + LANES), BF16)
    sent = pl.pallas_call(
        pack_kernel,
        out_shape=row,
        in_specs=hbm_specs(5),
        out_specs=vmem_specs(1)[0],
        scratch_shapes=[
            pltpu.VMEM((top, group_size), jnp.int32),
            pltpu.VMEM((top, group_size), jnp.int32),
            pltpu.VMEM((top, group_size), F32),
            pltpu.SemaphoreType.DMA((5,)),
        ],
        compiler_params=pltpu.CompilerParams(vmem_limit_bytes=2 * 2**20),
        name="pack",
    )(*inputs)
    held_weights = pl.pallas_call(
        functools.partial(fetch_kernel, ready),
        out_shape=[held] * 2,
        in_specs=hbm_specs(2),
        out_specs=vmem_specs(2),
        scratch_shapes=[pltpu.SemaphoreType.DMA((experts, 2))],
        compiler_params=pltpu.CompilerParams(vmem_limit_bytes=2**20),
        name="fetch",
    )(*weights[:2])
    blocks = devices // 2
    kept = [pltpu.with_memory_space_constraint(w, pltpu.VMEM) for w in held_weights]
    near_rows, *held_weights = pl.pallas_call(
        join_kernel,
        out_shape=[jax.ShapeDtypeStruct((rows // 2, 2 * width + LANES), BF16)] + [held] * 2,
        in_specs=vmem_specs(blocks + 2),
        out_specs=vmem_specs(3),
        input_output_aliases={blocks: 1, blocks + 1: 2},
        compiler_params=pltpu.CompilerParams(vmem_limit_bytes=2 * 2**20),
        name="join",
    )(sent, *[swap(sent, 2 * k) for k in range(1, blocks)], *kept)
    far_rows = swap(near_rows, 1)

    pack_rows = slots // LANES * hidden + (width // replicas // LANES + 1) * rows
    half = jax.ShapeDtypeStruct((rows // 2, 2 * width), BF16)
    pack = jax.ShapeDtypeStruct((pack_rows, LANES), BF16)
    kept = [pltpu.with_memory_space_constraint(w, pltpu.VMEM) for w in held_weights]
    lead = min(LEAD, experts)
    slot_wide = jax.ShapeDtypeStruct((slots, width), BF16)
    slot_narrow = jax.ShapeDtypeStruct((slots, hidden), F32)
    outs = pl.pallas_call(
        functools.partial(
            activations_kernel, (top, capacity, groups, tensor, replicas), ready, lead
        ),
        out_shape=[held] * 3
        + [
            jax.ShapeDtypeStruct((slots, hidden), BF16),
            slot_narrow,
            slot_narrow,
            slot_wide,
            jax.ShapeDtypeStruct((rows, slots), BF16),
            jax.ShapeDtypeStruct((slots, 1), F32),
        ]
        + [pack] * replicas,
        in_specs=vmem_specs(2) + hbm_specs(3) + vmem_specs(2),
        out_specs=vmem_specs(9 + replicas),
        scratch_shapes=[
            pltpu.VMEM((slots, width), BF16),
            pltpu.SemaphoreType.DMA((experts, 2)),
            pltpu.SemaphoreType.DMA((experts, 1)),
        ],
        input_output_aliases={5: 0, 6: 1},
        compiler_params=pltpu.CompilerParams(vmem_limit_bytes=6 * 2**20),
        cost_estimate=pl.CostEstimate(
            flops=4 * slots * hidden * width,
            bytes_accessed=4 * experts * hidden * width,
            transcendentals=slots * hidden,
        ),
        name="activations",
    )(near_rows, far_rows, *weights, *kept)
    kept = [pltpu.with_memory_space_constraint(w, pltpu.VMEM) for w in outs[:3]]
    packs = outs[9:]
    side = jax.ShapeDtypeStruct((rows // 2, width), BF16)
    keep, send_one, send_two, _ = pl.pallas_call(
        functools.partial(outputs_kernel, lead),
        out_shape=[half, side, side, held],
        in_specs=vmem_specs(9) + hbm_specs(1),
        out_specs=vmem_specs(4),
        scratch_shapes=[
            pltpu.VMEM((slots, 2 * width), BF16),
            pltpu.VMEM((2, slots, hidden), BF16),
            pltpu.SemaphoreType.DMA((experts, 1)),
        ],
        input_output_aliases={8: 3},
        compiler_params=pltpu.CompilerParams(vmem_limit_bytes=6 * 2**20),
        cost_estimate=pl.CostEstimate(
            flops=8 * slots * hidden * width,
            bytes_accessed=6 * experts * hidden * width,
            transcendentals=0,
        ),
        name="outputs",
    )(*outs[3:9], *kept, weights[2])

    own, *others_near = pl.pallas_call(
        functools.partial(near_kernel, mine),
        out_shape=[jax.ShapeDtypeStruct((mine, 2 * width), F32)]
        + [jax.ShapeDtypeStruct((mine, 2 * width), BF16)] * (devices // 2 - 1),
        in_specs=vmem_specs(3),
        out_specs=vmem_specs(devices // 2),
        compiler_params=pltpu.CompilerParams(vmem_limit_bytes=2 * 2**20),
        name="near",
    )(keep, swap(send_one, 1), swap(send_two, 1))
    received = [swap(part, 2 * k) for k, part in enumerate(others_near, 1)]

    arrived = [packs[0]]
    for k in range(1, replicas):
        arrived.append(lax.ppermute(packs[k], "dp", [(i, i ^ k) for i in range(replicas)]))
    share = width // replicas
    grad, total = pl.pallas_call(
        functools.partial(grad_kernel, (top, capacity, groups, tensor, replicas)),
        out_shape=[
            jax.ShapeDtypeStruct((experts, hidden, share), BF16),
            jax.ShapeDtypeStruct((mine, 2 * width), F32),
        ],
        in_specs=vmem_specs(replicas + 1),
        out_specs=[pl.BlockSpec(memory_space=pl.ANY)] + vmem_specs(1),
        scratch_shapes=[
            pltpu.VMEM((replicas * slots, share), BF16),
            pltpu.VMEM((hidden, replicas * slots), BF16),
            pltpu.VMEM((experts, hidden, share), BF16),
            pltpu.SemaphoreType.DMA((experts,)),
        ],
        compiler_params=pltpu.CompilerParams(vmem_limit_bytes=10 * 2**20),
        cost_estimate=pl.CostEstimate(
            flops=2 * replicas * slots * share * hidden,
            bytes_accessed=2 * experts * share * hidden,
            transcendentals=0,
        ),
        name="grad_down",
    )(*arrived, own)
    for part in received:
        total = total + part.astype(F32)
    total = total.astype(BF16)
    return (total[:, :width], total[:, width:], jnp.swapaxes(grad, 1, 2))


def solution(mesh):
    return jax.shard_map(
        shards,
        mesh=mesh,
        in_specs=(
            P(("dp", "expert", "tensor"), None),
            P(("dp", "expert"), None),
            P(("dp", "expert"), None),
            P(("dp", "expert"), None),
            P(("dp", "expert", "tensor"), None),
            P("expert", None, "tensor"),
            P("expert", None, "tensor"),
            P("expert", None, "tensor"),
        ),
        out_specs=(
            P(("dp", "expert", "tensor"), None),
            P(("dp", "expert", "tensor"), None),
            P("expert", "dp", "tensor"),
        ),
        check_vma=False,
    )
```

```python
import functools

import jax
import jax.numpy as jnp
from jax import lax
from jax.experimental import pallas as pl
from jax.experimental.pallas import tpu as pltpu
from jax.sharding import PartitionSpec as P

F32 = jnp.float32
BF16 = jnp.bfloat16
LANES = 128
EARLY = 3
LEAD = 4
NT = (((1,), (1,)), ((), ()))
TN = (((0,), (0,)), ((), ()))


def whole_part(values, divisor):
    return jnp.floor((values + 0.5) * (1.0 / divisor))


def fiota(shape, axis):
    return lax.broadcasted_iota(jnp.int32, shape, axis).astype(F32)


def row_tokens(rows, devices, tensor):
    device = lax.axis_index("expert") * tensor + lax.axis_index("tensor")
    pair = lax.div(device, 2)
    parity = device - pair * 2
    mine = rows // devices
    row = lax.broadcasted_iota(jnp.int32, (rows, 1), 0)
    second = jnp.where(row >= rows // 2, 1, 0)
    within = row - second * (rows // 2)
    block = lax.div(within, jnp.full_like(within, mine))
    token = (block ^ pair) * (2 * mine) + (second ^ parity) * mine + within - block * mine
    return token.astype(F32)


def slot_tables(routing, token, top, first_expert, capacity, groups, slots):
    rows = routing.shape[0]
    lane = fiota((rows, slots), 1)
    expert = whole_part(lane, groups * capacity)
    inner = lane - expert * (groups * capacity)
    group = whole_part(inner, capacity)
    target = (expert + first_expert) * capacity + inner - group * capacity
    target = jnp.where(whole_part(token, rows // groups) == group, target, -1.0)
    names = routing[:, :top] * float(capacity) + routing[:, top : 2 * top]
    weights = routing[:, 2 * top : 3 * top] + routing[:, 3 * top : 4 * top]
    chosen = jnp.zeros((rows, slots), F32)
    gains = jnp.zeros((rows, slots), F32)
    for k in range(top):
        match = names[:, k : k + 1] == target
        chosen = chosen + jnp.where(match, 1.0, 0.0)
        gains = gains + jnp.where(match, weights[:, k : k + 1], 0.0)
    return chosen, gains


def column_blocks(width):
    return [(at, min(LANES, width - at)) for at in range(0, width, LANES)]


def fetch_experts(weights, held, sems, first, last):
    return [
        pltpu.make_async_copy(source.at[e], target.at[e], sems.at[e, i])
        for e in range(first, last)
        for i, (source, target) in enumerate(zip(weights, held))
    ]


def pack_kernel(*refs):
    sources, out_ref = refs[:5], refs[5]
    routes_ref, positions_ref, weights_ref, sems = refs[6:]
    mine, width = sources[0].shape
    top, group_size = routes_ref.shape
    targets = (
        out_ref.at[:, :width],
        out_ref.at[:, width : 2 * width],
        routes_ref,
        positions_ref,
        weights_ref,
    )
    copies = [
        pltpu.make_async_copy(source, target, sems.at[i])
        for i, (source, target) in enumerate(zip(sources, targets))
    ]
    for copy in copies:
        copy.start()
    for copy in copies:
        copy.wait()
    weights = weights_ref[...]
    high = weights.astype(BF16)
    low = (weights - high.astype(F32)).astype(BF16)
    table = jnp.concatenate(
        [routes_ref[...].astype(F32), positions_ref[...].astype(F32), high.astype(F32), low.astype(F32)],
        axis=0,
    ).astype(BF16)
    first = lax.axis_index("tensor") * mine
    column = lax.broadcasted_iota(jnp.int32, (mine, group_size), 1)
    row = lax.broadcasted_iota(jnp.int32, (mine, group_size), 0)
    pick = jnp.where(column == row + first, 1.0, 0.0).astype(BF16)
    routing = lax.dot_general(pick, table, NT, preferred_element_type=F32)
    out_ref[:, 2 * width :] = jnp.concatenate(
        [routing, jnp.zeros((mine, LANES - 4 * top), F32)], axis=1
    ).astype(BF16)


def join_kernel(*refs):
    out_ref = refs[-3]
    mine = refs[0].shape[0]
    for k, block in enumerate(refs[:-5]):
        out_ref[k * mine : (k + 1) * mine, :] = block[...]


def fetch_kernel(last, *refs):
    weights, held, sems = refs[:2], refs[2:4], refs[4]
    copies = fetch_experts(weights, held, sems, 0, last)
    for copy in copies:
        copy.start()
    for copy in copies:
        copy.wait()


def activations_kernel(
    sizes, ready, lead, x_ref, far_ref, gate_hbm, up_hbm, down_hbm, *rest
):
    top, capacity, groups, tensor, replicas = sizes
    gate_w, up_w, down_w, activations, slope_ref, swish_ref, grads_ref, picker_ref, gain_ref = rest[2:11]
    packs = rest[11 : 11 + replicas]
    filled, sems, down_sems = rest[11 + replicas :]
    experts, hidden, width = gate_hbm.shape
    half = x_ref.shape[0]
    rows = 2 * half
    slots = filled.shape[0]
    per_expert = slots // experts
    batches = [
        fetch_experts((gate_hbm, up_hbm), (gate_w, up_w), sems, first, min(first + 2, experts))
        for first in range(ready, experts, 2)
    ]
    downs = fetch_experts((down_hbm,), (down_w,), down_sems, 0, lead)
    for copy in sum(batches[:2], []):
        copy.start()

    first_expert = (lax.axis_index("expert") * experts).astype(F32)
    routing = jnp.concatenate([x_ref[:, 2 * width :], far_ref[:, 2 * width :]], axis=0).astype(F32)
    token = row_tokens(rows, groups * tensor, tensor)
    chosen, gains = slot_tables(routing, token, top, first_expert, capacity, groups, slots)
    scatter = chosen.T.astype(BF16)
    gain = jnp.sum(gains.T, axis=1, keepdims=True)
    gain_ref[...] = gain
    picker_ref[...] = chosen.astype(BF16)
    step = min(512, width)
    for at in range(0, 2 * width, step):
        given = jnp.concatenate([x_ref[:, at : at + step], far_ref[:, at : at + step]], axis=0)
        slot_rows = jnp.dot(scatter, given, preferred_element_type=F32)
        if at < width:
            filled[:, at : at + step] = slot_rows.astype(BF16)
        else:
            grads_ref[:, at - width : at - width + step] = (gain * slot_rows).astype(BF16)

    for e in range(experts):
        if e >= ready and (e - ready) % 2 == 0:
            at = (e - ready) // 2
            for copy in batches[at]:
                copy.wait()
            for copy in batches[at + 2] if at + 2 < len(batches) else []:
                copy.start()
            if at + 3 == len(batches):
                for copy in downs:
                    copy.start()
        here = slice(e * per_expert, (e + 1) * per_expert)
        slot_rows = filled[here, :]
        gate_pre = lax.dot_general(slot_rows, gate_w[e], NT, preferred_element_type=F32)
        up_pre = lax.dot_general(slot_rows, up_w[e], NT, preferred_element_type=F32)
        squash = 1.0 / (1.0 + jnp.exp(-gate_pre))
        swish = gate_pre * squash
        activations[here, :] = (swish * up_pre).astype(BF16)
        slope_ref[here, :] = up_pre * squash * (1.0 + gate_pre * (1.0 - squash))
        swish_ref[here, :] = swish
    if len(batches) < 3:
        for copy in downs:
            copy.start()

    replica = lax.axis_index("dp")
    share = width // replicas
    turned = {
        (block, lane): activations[block : block + LANES, lane : lane + size].T
        for block in range(0, slots, LANES)
        for lane, size in column_blocks(hidden)
    }
    for k in range(replicas):
        peer = replica ^ k
        at = 0
        for block in range(0, slots, LANES):
            for lane, size in column_blocks(hidden):
                packs[k][at : at + size, :] = turned[block, lane]
                at += size
        for lane in range(0, share, LANES):
            column = pl.multiple_of(width + peer * share + lane, LANES)
            packs[k][at : at + half, :] = x_ref[:, pl.ds(column, LANES)]
            packs[k][at + half : at + rows, :] = far_ref[:, pl.ds(column, LANES)]
            at += rows
        packs[k][at : at + half, :] = x_ref[:, 2 * width :]
        packs[k][at + half : at + rows, :] = far_ref[:, 2 * width :]
    for copy in downs:
        copy.wait()


def outputs_kernel(
    lead, activations, slope_ref, swish_ref, grads_ref, picker_ref, gain_ref, gate_w, up_w, unused, down_hbm,
    keep_ref, send_one, send_two, down_w, results, backs, sems
):
    experts, _, width = gate_w.shape
    half = keep_ref.shape[0]
    slots = activations.shape[0]
    per_expert = slots // experts
    copies = fetch_experts((down_hbm,), (down_w,), sems, lead, experts)
    for copy in copies:
        copy.start()
    def last_products(e):
        here = slice(e * per_expert, (e + 1) * per_expert)
        results[here, width:] = (
            jnp.dot(backs[0, here, :], gate_w[e], preferred_element_type=F32)
            + jnp.dot(backs[1, here, :], up_w[e], preferred_element_type=F32)
        ).astype(BF16)

    for e in range(experts):
        if e >= lead and (e - lead) % 2 == 0:
            for copy in copies[e - lead : e - lead + 2]:
                copy.wait()
        here = slice(e * per_expert, (e + 1) * per_expert)
        act_grad = lax.dot_general(grads_ref[here, :], down_w[e], NT, preferred_element_type=F32)
        backs[0, here, :] = (act_grad * slope_ref[here, :]).astype(BF16)
        backs[1, here, :] = (act_grad * swish_ref[here, :]).astype(BF16)
        forward = jnp.dot(activations[here, :], down_w[e], preferred_element_type=F32)
        results[here, :width] = (forward.astype(BF16).astype(F32) * gain_ref[here, :]).astype(BF16)
        if e > 0:
            last_products(e - 1)
    last_products(experts - 1)

    step = min(512, width)
    for at in range(0, 2 * width, step):
        total = jnp.dot(picker_ref[...], results[:, at : at + step], preferred_element_type=F32)
        keep_ref[:, at : at + step] = total[:half].astype(BF16)
        send_ref = send_one if at < width else send_two
        to = at % width
        send_ref[:, to : to + step] = total[half:].astype(BF16)


def grad_kernel(sizes, *refs):
    top, capacity, groups, tensor, replicas = sizes
    packs = refs[:replicas]
    own_ref, out_hbm, own_out, grads, acts, result, sems = refs[replicas:]
    experts, hidden, share = out_hbm.shape
    per_replica = groups * capacity
    slots = experts * per_replica
    per_expert = replicas * per_replica
    act_rows = slots // LANES * hidden
    rows = (packs[0].shape[0] - act_rows) // (share // LANES + 1)

    first_expert = (lax.axis_index("expert") * experts).astype(F32)
    token = row_tokens(rows, groups * tensor, tensor)
    for k in range(replicas):
        at = act_rows
        routing = packs[k][at + (share // LANES) * rows :, :].astype(F32)
        chosen, gains = slot_tables(
            routing, token, top, first_expert, capacity, groups, slots
        )
        scatter = chosen.T.astype(BF16)
        gain = jnp.sum(gains.T, axis=1, keepdims=True)
        for lane in range(0, share, LANES):
            filled = jnp.dot(scatter, packs[k][at : at + rows, :], preferred_element_type=F32)
            filled = (gain * filled).astype(BF16)
            for e in range(experts):
                to = e * per_expert + k * per_replica
                grads[to : to + per_replica, lane : lane + LANES] = filled[
                    e * per_replica : (e + 1) * per_replica
                ]
            at += rows

    left = jnp.concatenate(
        [
            packs[k][block * hidden : (block + 1) * hidden, :]
            for k in range(replicas)
            for block in range(slots // LANES)
        ],
        axis=1,
    )
    if experts > 1:
        lanes = replicas * slots
        before = fiota((lanes, lanes), 0)
        after = fiota((lanes, lanes), 1)
        source = whole_part(before, slots)
        inner = before - source * slots
        expert = whole_part(inner, per_replica)
        place = expert * per_expert + source * per_replica + inner - expert * per_replica
        order = jnp.where(place == after, 1.0, 0.0).astype(BF16)
        left = jnp.dot(left, order, preferred_element_type=F32).astype(BF16)
    acts[...] = left

    own_out[...] = own_ref[...].astype(F32)

    copies = []
    for e in range(experts):
        low = e * per_expert // LANES * LANES
        high = -(-(e + 1) * per_expert // LANES) * LANES
        right = grads[low:high, :]
        if high - low > per_expert:
            row = lax.broadcasted_iota(jnp.int32, right.shape, 0) + low
            inside = (row >= e * per_expert) & (row < (e + 1) * per_expert)
            right = jnp.where(inside, right.astype(F32), 0.0).astype(BF16)
        total = jnp.dot(acts[:, low:high], right, preferred_element_type=F32)
        result[e] = (total * (1.0 / replicas)).astype(BF16)
        copies.append(pltpu.make_async_copy(result.at[e], out_hbm.at[e], sems.at[e]))
        copies[-1].start()
    for copy in copies:
        copy.wait()


def near_kernel(mine, keep_ref, one_ref, two_ref, own_ref, *parts):
    width = one_ref.shape[1]
    for k, part in enumerate((own_ref, *parts)):
        here = slice(k * mine, (k + 1) * mine)
        for side, ref in enumerate((one_ref, two_ref)):
            columns = slice(side * width, (side + 1) * width)
            part[:, columns] = (
                keep_ref[here, columns].astype(F32) + ref[here, :].astype(F32)
            ).astype(part.dtype)


def hbm_specs(count):
    return [pl.BlockSpec(memory_space=pltpu.HBM)] * count


def vmem_specs(count):
    return [pl.BlockSpec(memory_space=pltpu.VMEM)] * count


def shards(
    tokens, routes, positions, combine_weights, cotangent, gate_weight, up_weight, down_weight
):
    experts, width, hidden = gate_weight.shape
    replicas = lax.axis_size("dp")
    groups = lax.axis_size("expert")
    tensor = lax.axis_size("tensor")
    group_size, top = routes.shape
    capacity = group_size // 2
    slots = experts * groups * capacity
    mine = tokens.shape[0]
    devices = groups * tensor
    rows = mine * devices
    both = ("expert", "tensor")

    def swap(values, distance):
        return lax.ppermute(values, both, [(i, i ^ distance) for i in range(devices)])

    weights = [
        pltpu.with_memory_space_constraint(jnp.swapaxes(w, 1, 2), pltpu.HBM)
        for w in (gate_weight, up_weight, down_weight)
    ]
    held = pltpu.VMEM((experts, hidden, width), BF16)
    ready = min(EARLY, experts)
    inputs = [
        pltpu.with_memory_space_constraint(x, pltpu.HBM)
        for x in (tokens, cotangent, routes.T, positions.T, combine_weights.T)
    ]
    row = jax.ShapeDtypeStruct((mine, 2 * width + LANES), BF16)
    sent = pl.pallas_call(
        pack_kernel,
        out_shape=row,
        in_specs=hbm_specs(5),
        out_specs=vmem_specs(1)[0],
        scratch_shapes=[
            pltpu.VMEM((top, group_size), jnp.int32),
            pltpu.VMEM((top, group_size), jnp.int32),
            pltpu.VMEM((top, group_size), F32),
            pltpu.SemaphoreType.DMA((5,)),
        ],
        compiler_params=pltpu.CompilerParams(vmem_limit_bytes=2 * 2**20),
        name="pack",
    )(*inputs)
    held_weights = pl.pallas_call(
        functools.partial(fetch_kernel, ready),
        out_shape=[held] * 2,
        in_specs=hbm_specs(2),
        out_specs=vmem_specs(2),
        scratch_shapes=[pltpu.SemaphoreType.DMA((experts, 2))],
        compiler_params=pltpu.CompilerParams(vmem_limit_bytes=2**20),
        name="fetch",
    )(*weights[:2])
    blocks = devices // 2
    kept = [pltpu.with_memory_space_constraint(w, pltpu.VMEM) for w in held_weights]
    near_rows, *held_weights = pl.pallas_call(
        join_kernel,
        out_shape=[jax.ShapeDtypeStruct((rows // 2, 2 * width + LANES), BF16)] + [held] * 2,
        in_specs=vmem_specs(blocks + 2),
        out_specs=vmem_specs(3),
        input_output_aliases={blocks: 1, blocks + 1: 2},
        compiler_params=pltpu.CompilerParams(vmem_limit_bytes=2 * 2**20),
        name="join",
    )(sent, *[swap(sent, 2 * k) for k in range(1, blocks)], *kept)
    far_rows = swap(near_rows, 1)

    pack_rows = slots // LANES * hidden + (width // replicas // LANES + 1) * rows
    half = jax.ShapeDtypeStruct((rows // 2, 2 * width), BF16)
    pack = jax.ShapeDtypeStruct((pack_rows, LANES), BF16)
    kept = [pltpu.with_memory_space_constraint(w, pltpu.VMEM) for w in held_weights]
    lead = min(LEAD, experts)
    slot_wide = jax.ShapeDtypeStruct((slots, width), BF16)
    slot_narrow = jax.ShapeDtypeStruct((slots, hidden), F32)
    outs = pl.pallas_call(
        functools.partial(
            activations_kernel, (top, capacity, groups, tensor, replicas), ready, lead
        ),
        out_shape=[held] * 3
        + [
            jax.ShapeDtypeStruct((slots, hidden), BF16),
            slot_narrow,
            slot_narrow,
            slot_wide,
            jax.ShapeDtypeStruct((rows, slots), BF16),
            jax.ShapeDtypeStruct((slots, 1), F32),
        ]
        + [pack] * replicas,
        in_specs=vmem_specs(2) + hbm_specs(3) + vmem_specs(2),
        out_specs=vmem_specs(9 + replicas),
        scratch_shapes=[
            pltpu.VMEM((slots, width), BF16),
            pltpu.SemaphoreType.DMA((experts, 2)),
            pltpu.SemaphoreType.DMA((experts, 1)),
        ],
        input_output_aliases={5: 0, 6: 1},
        compiler_params=pltpu.CompilerParams(vmem_limit_bytes=6 * 2**20),
        cost_estimate=pl.CostEstimate(
            flops=4 * slots * hidden * width,
            bytes_accessed=4 * experts * hidden * width,
            transcendentals=slots * hidden,
        ),
        name="activations",
    )(near_rows, far_rows, *weights, *kept)
    kept = [pltpu.with_memory_space_constraint(w, pltpu.VMEM) for w in outs[:3]]
    packs = outs[9:]
    side = jax.ShapeDtypeStruct((rows // 2, width), BF16)
    keep, send_one, send_two, _ = pl.pallas_call(
        functools.partial(outputs_kernel, lead),
        out_shape=[half, side, side, held],
        in_specs=vmem_specs(9) + hbm_specs(1),
        out_specs=vmem_specs(4),
        scratch_shapes=[
            pltpu.VMEM((slots, 2 * width), BF16),
            pltpu.VMEM((2, slots, hidden), BF16),
            pltpu.SemaphoreType.DMA((experts, 1)),
        ],
        input_output_aliases={8: 3},
        compiler_params=pltpu.CompilerParams(vmem_limit_bytes=6 * 2**20),
        cost_estimate=pl.CostEstimate(
            flops=8 * slots * hidden * width,
            bytes_accessed=6 * experts * hidden * width,
            transcendentals=0,
        ),
        name="outputs",
    )(*outs[3:9], *kept, weights[2])

    own, *others_near = pl.pallas_call(
        functools.partial(near_kernel, mine),
        out_shape=[jax.ShapeDtypeStruct((mine, 2 * width), F32)]
        + [jax.ShapeDtypeStruct((mine, 2 * width), BF16)] * (devices // 2 - 1),
        in_specs=vmem_specs(3),
        out_specs=vmem_specs(devices // 2),
        compiler_params=pltpu.CompilerParams(vmem_limit_bytes=2 * 2**20),
        name="near",
    )(keep, swap(send_one, 1), swap(send_two, 1))
    received = [swap(part, 2 * k) for k, part in enumerate(others_near, 1)]

    arrived = [packs[0]]
    for k in range(1, replicas):
        arrived.append(lax.ppermute(packs[k], "dp", [(i, i ^ k) for i in range(replicas)]))
    share = width // replicas
    grad, total = pl.pallas_call(
        functools.partial(grad_kernel, (top, capacity, groups, tensor, replicas)),
        out_shape=[
            jax.ShapeDtypeStruct((experts, hidden, share), BF16),
            jax.ShapeDtypeStruct((mine, 2 * width), F32),
        ],
        in_specs=vmem_specs(replicas + 1),
        out_specs=[pl.BlockSpec(memory_space=pl.ANY)] + vmem_specs(1),
        scratch_shapes=[
            pltpu.VMEM((replicas * slots, share), BF16),
            pltpu.VMEM((hidden, replicas * slots), BF16),
            pltpu.VMEM((experts, hidden, share), BF16),
            pltpu.SemaphoreType.DMA((experts,)),
        ],
        compiler_params=pltpu.CompilerParams(vmem_limit_bytes=10 * 2**20),
        cost_estimate=pl.CostEstimate(
            flops=2 * replicas * slots * share * hidden,
            bytes_accessed=2 * experts * share * hidden,
            transcendentals=0,
        ),
        name="grad_down",
    )(*arrived, own)
    total = (total + sum(part.astype(F32) for part in received[::-1])).astype(BF16)
    return (total[:, :width], total[:, width:], jnp.swapaxes(grad, 1, 2))


def solution(mesh):
    return jax.shard_map(
        shards,
        mesh=mesh,
        in_specs=(
            P(("dp", "expert", "tensor"), None),
            P(("dp", "expert"), None),
            P(("dp", "expert"), None),
            P(("dp", "expert"), None),
            P(("dp", "expert", "tensor"), None),
            P("expert", None, "tensor"),
            P("expert", None, "tensor"),
            P("expert", None, "tensor"),
        ),
        out_specs=(
            P(("dp", "expert", "tensor"), None),
            P(("dp", "expert", "tensor"), None),
            P("expert", "dp", "tensor"),
        ),
        check_vma=False,
    )
```

```python
import functools

import jax
import jax.numpy as jnp
from jax import lax
from jax.experimental import pallas as pl
from jax.experimental.pallas import tpu as pltpu
from jax.sharding import PartitionSpec as P

F32 = jnp.float32
BF16 = jnp.bfloat16
LANES = 128
EARLY = 3
TURNED = 2
LEAD = 4
NT = (((1,), (1,)), ((), ()))
TN = (((0,), (0,)), ((), ()))


def whole_part(values, divisor):
    return jnp.floor((values + 0.5) * (1.0 / divisor))


def fiota(shape, axis):
    return lax.broadcasted_iota(jnp.int32, shape, axis).astype(F32)


def row_tokens(rows, devices, tensor):
    device = lax.axis_index("expert") * tensor + lax.axis_index("tensor")
    pair = lax.div(device, 2)
    parity = device - pair * 2
    mine = rows // devices
    row = lax.broadcasted_iota(jnp.int32, (rows, 1), 0)
    second = jnp.where(row >= rows // 2, 1, 0)
    within = row - second * (rows // 2)
    block = lax.div(within, jnp.full_like(within, mine))
    token = (block ^ pair) * (2 * mine) + (second ^ parity) * mine + within - block * mine
    return token.astype(F32)


def slot_tables(routing, token, top, first_expert, capacity, groups, slots):
    rows = routing.shape[0]
    lane = fiota((rows, slots), 1)
    expert = whole_part(lane, groups * capacity)
    inner = lane - expert * (groups * capacity)
    group = whole_part(inner, capacity)
    target = (expert + first_expert) * capacity + inner - group * capacity
    target = jnp.where(whole_part(token, rows // groups) == group, target, -1.0)
    names = routing[:, :top] * float(capacity) + routing[:, top : 2 * top]
    weights = routing[:, 2 * top : 3 * top] + routing[:, 3 * top : 4 * top]
    chosen = jnp.zeros((rows, slots), F32)
    gains = jnp.zeros((rows, slots), F32)
    for k in range(top):
        match = names[:, k : k + 1] == target
        chosen = chosen + jnp.where(match, 1.0, 0.0)
        gains = gains + jnp.where(match, weights[:, k : k + 1], 0.0)
    return chosen, gains


def column_blocks(width):
    return [(at, min(LANES, width - at)) for at in range(0, width, LANES)]


def fetch_experts(weights, held, sems, first, last):
    return [
        pltpu.make_async_copy(source.at[e], target.at[e], sems.at[e, i])
        for e in range(first, last)
        for i, (source, target) in enumerate(zip(weights, held))
    ]


def turn_block(source, target, part, parts):
    size = source.shape[1] // parts
    for at in range(part * size, (part + 1) * size, LANES):
        target[at : at + LANES, :] = source[:, at : at + LANES].T


def pack_kernel(*refs):
    sources, out_ref = refs[:5], refs[5]
    routes_ref, positions_ref, weights_ref, sems = refs[6:]
    mine, width = sources[0].shape
    top, group_size = routes_ref.shape
    targets = (
        out_ref.at[:, :width],
        out_ref.at[:, width : 2 * width],
        routes_ref,
        positions_ref,
        weights_ref,
    )
    copies = [
        pltpu.make_async_copy(source, target, sems.at[i])
        for i, (source, target) in enumerate(zip(sources, targets))
    ]
    for copy in copies:
        copy.start()
    for copy in copies:
        copy.wait()
    weights = weights_ref[...]
    high = weights.astype(BF16)
    low = (weights - high.astype(F32)).astype(BF16)
    table = jnp.concatenate(
        [routes_ref[...].astype(F32), positions_ref[...].astype(F32), high.astype(F32), low.astype(F32)],
        axis=0,
    ).astype(BF16)
    first = lax.axis_index("tensor") * mine
    column = lax.broadcasted_iota(jnp.int32, (mine, group_size), 1)
    row = lax.broadcasted_iota(jnp.int32, (mine, group_size), 0)
    pick = jnp.where(column == row + first, 1.0, 0.0).astype(BF16)
    routing = lax.dot_general(pick, table, NT, preferred_element_type=F32)
    out_ref[:, 2 * width :] = jnp.concatenate(
        [routing, jnp.zeros((mine, LANES - 4 * top), F32)], axis=1
    ).astype(BF16)


def join_kernel(*refs):
    out_ref = refs[-3]
    mine = refs[0].shape[0]
    for k, block in enumerate(refs[:-5]):
        out_ref[k * mine : (k + 1) * mine, :] = block[...]


def fetch_kernel(last, *refs):
    weights, held, sems = refs[:2], refs[2:4], refs[4]
    copies = fetch_experts(weights, held, sems, 0, last)
    for copy in copies:
        copy.start()
    for copy in copies:
        copy.wait()


def activations_kernel(
    sizes, ready, lead, x_ref, far_ref, gate_hbm, up_hbm, down_hbm, *rest
):
    top, capacity, groups, tensor, replicas = sizes
    gate_w, up_w, down_w, activations, slope_ref, swish_ref, grads_ref, picker_ref, gain_ref = rest[2:11]
    packs = rest[11 : 11 + replicas]
    filled, sems, down_sems = rest[11 + replicas :]
    experts, hidden, width = gate_hbm.shape
    half = x_ref.shape[0]
    rows = 2 * half
    slots = filled.shape[0]
    per_expert = slots // experts
    batches = [
        fetch_experts((gate_hbm, up_hbm), (gate_w, up_w), sems, first, min(first + 2, experts))
        for first in range(ready, experts, 2)
    ]
    downs = fetch_experts((down_hbm,), (down_w,), down_sems, 0, lead)
    for copy in sum(batches[:2], []) + (downs if len(batches) < 3 else []):
        copy.start()

    first_expert = (lax.axis_index("expert") * experts).astype(F32)
    routing = jnp.concatenate([x_ref[:, 2 * width :], far_ref[:, 2 * width :]], axis=0).astype(F32)
    token = row_tokens(rows, groups * tensor, tensor)
    chosen, gains = slot_tables(routing, token, top, first_expert, capacity, groups, slots)
    scatter = chosen.T.astype(BF16)
    gain = jnp.sum(gains.T, axis=1, keepdims=True)
    gain_ref[...] = gain
    picker_ref[...] = chosen.astype(BF16)
    step = min(512, width)
    for at in range(0, 2 * width, step):
        given = jnp.concatenate([x_ref[:, at : at + step], far_ref[:, at : at + step]], axis=0)
        slot_rows = jnp.dot(scatter, given, preferred_element_type=F32)
        if at < width:
            filled[:, at : at + step] = slot_rows.astype(BF16)
        else:
            grads_ref[:, at - width : at - width + step] = (gain * slot_rows).astype(BF16)

    for e in range(experts):
        if e >= ready and (e - ready) % 2 == 0:
            at = (e - ready) // 2
            for copy in batches[at]:
                copy.wait()
            for copy in batches[at + 2] if at + 2 < len(batches) else []:
                copy.start()
            if at + 3 == len(batches):
                for copy in downs:
                    copy.start()
        here = slice(e * per_expert, (e + 1) * per_expert)
        slot_rows = filled[here, :]
        gate_pre = lax.dot_general(slot_rows, gate_w[e], NT, preferred_element_type=F32)
        up_pre = lax.dot_general(slot_rows, up_w[e], NT, preferred_element_type=F32)
        squash = 1.0 / (1.0 + jnp.exp(-gate_pre))
        swish = gate_pre * squash
        activations[here, :] = (swish * up_pre).astype(BF16)
        slope_ref[here, :] = up_pre * squash * (1.0 + gate_pre * (1.0 - squash))
        swish_ref[here, :] = swish
    replica = lax.axis_index("dp")
    share = width // replicas
    turned = {
        (block, lane): activations[block : block + LANES, lane : lane + size].T
        for block in range(0, slots, LANES)
        for lane, size in column_blocks(hidden)
    }
    for k in range(replicas):
        peer = replica ^ k
        at = 0
        for block in range(0, slots, LANES):
            for lane, size in column_blocks(hidden):
                packs[k][at : at + size, :] = turned[block, lane]
                at += size
        for lane in range(0, share, LANES):
            column = pl.multiple_of(width + peer * share + lane, LANES)
            packs[k][at : at + half, :] = x_ref[:, pl.ds(column, LANES)]
            packs[k][at + half : at + rows, :] = far_ref[:, pl.ds(column, LANES)]
            at += rows
        packs[k][at : at + half, :] = x_ref[:, 2 * width :]
        packs[k][at + half : at + rows, :] = far_ref[:, 2 * width :]
    for copy in downs:
        copy.wait()


def outputs_kernel(
    lead, activations, slope_ref, swish_ref, grads_ref, picker_ref, gain_ref, gate_w, up_w, unused, down_hbm,
    keep_ref, send_one, send_two, down_w, results, backs, turned, sems
):
    experts, _, width = gate_w.shape
    half = keep_ref.shape[0]
    slots = activations.shape[0]
    per_expert = slots // experts
    copies = fetch_experts((down_hbm,), (down_w,), sems, lead, experts)
    for copy in copies:
        copy.start()
    def arrive(e):
        if e >= lead and (e - lead) % 2 == 0:
            for copy in copies[e - lead : e - lead + 2]:
                copy.wait()

    def turn(e, part):
        if e < experts:
            turn_block(down_w.at[e], turned.at[e % TURNED], part, 4)

    def place(e):
        return slice(e * per_expert, (e + 1) * per_expert)

    arrive(0)
    for e in range(experts + 1):
        arrive(e + 1)
        turn(e + 1, 0)
        if e < experts:
            here = place(e)
            if e > 0:
                act_grad = jnp.dot(grads_ref[here, :], turned[e % TURNED], preferred_element_type=F32)
            else:
                act_grad = lax.dot_general(
                    grads_ref[here, :], down_w[e], NT, preferred_element_type=F32
                )
            backs[0, here, :] = (act_grad * slope_ref[here, :]).astype(BF16)
            backs[1, here, :] = (act_grad * swish_ref[here, :]).astype(BF16)
        turn(e + 1, 1)
        if e < experts:
            forward = jnp.dot(activations[here, :], down_w[e], preferred_element_type=F32)
            results[here, :width] = (
                forward.astype(BF16).astype(F32) * gain_ref[here, :]
            ).astype(BF16)
        turn(e + 1, 2)
        if e > 0:
            there = place(e - 1)
            back = jnp.dot(backs[0, there, :], gate_w[e - 1], preferred_element_type=F32)
        turn(e + 1, 3)
        if e > 0:
            back = back + jnp.dot(backs[1, there, :], up_w[e - 1], preferred_element_type=F32)
            results[there, width:] = back.astype(BF16)

    step = min(512, width)
    for at in range(0, 2 * width, step):
        total = jnp.dot(picker_ref[...], results[:, at : at + step], preferred_element_type=F32)
        keep_ref[:, at : at + step] = total[:half].astype(BF16)
        send_ref = send_one if at < width else send_two
        to = at % width
        send_ref[:, to : to + step] = total[half:].astype(BF16)


def grad_kernel(sizes, *refs):
    top, capacity, groups, tensor, replicas = sizes
    packs = refs[:replicas]
    own_ref, out_hbm, own_out, grads, acts, result, sems = refs[replicas:]
    experts, hidden, share = out_hbm.shape
    per_replica = groups * capacity
    slots = experts * per_replica
    per_expert = replicas * per_replica
    act_rows = slots // LANES * hidden
    rows = (packs[0].shape[0] - act_rows) // (share // LANES + 1)

    first_expert = (lax.axis_index("expert") * experts).astype(F32)
    token = row_tokens(rows, groups * tensor, tensor)
    for k in range(replicas):
        at = act_rows
        routing = packs[k][at + (share // LANES) * rows :, :].astype(F32)
        chosen, gains = slot_tables(
            routing, token, top, first_expert, capacity, groups, slots
        )
        scatter = chosen.T.astype(BF16)
        gain = jnp.sum(gains.T, axis=1, keepdims=True)
        for lane in range(0, share, LANES):
            filled = jnp.dot(scatter, packs[k][at : at + rows, :], preferred_element_type=F32)
            filled = (gain * filled).astype(BF16)
            for e in range(experts):
                to = e * per_expert + k * per_replica
                grads[to : to + per_replica, lane : lane + LANES] = filled[
                    e * per_replica : (e + 1) * per_replica
                ]
            at += rows

    left = jnp.concatenate(
        [
            packs[k][block * hidden : (block + 1) * hidden, :]
            for k in range(replicas)
            for block in range(slots // LANES)
        ],
        axis=1,
    )
    if experts > 1:
        lanes = replicas * slots
        before = fiota((lanes, lanes), 0)
        after = fiota((lanes, lanes), 1)
        source = whole_part(before, slots)
        inner = before - source * slots
        expert = whole_part(inner, per_replica)
        place = expert * per_expert + source * per_replica + inner - expert * per_replica
        order = jnp.where(place == after, 1.0, 0.0).astype(BF16)
        left = jnp.dot(left, order, preferred_element_type=F32).astype(BF16)
    acts[...] = left

    own_out[...] = own_ref[...].astype(F32)

    copies = []
    for e in range(experts):
        low = e * per_expert // LANES * LANES
        high = -(-(e + 1) * per_expert // LANES) * LANES
        right = grads[low:high, :]
        if high - low > per_expert:
            row = lax.broadcasted_iota(jnp.int32, right.shape, 0) + low
            inside = (row >= e * per_expert) & (row < (e + 1) * per_expert)
            right = jnp.where(inside, right.astype(F32), 0.0).astype(BF16)
        total = jnp.dot(acts[:, low:high], right, preferred_element_type=F32)
        result[e] = (total * (1.0 / replicas)).astype(BF16)
        copies.append(pltpu.make_async_copy(result.at[e], out_hbm.at[e], sems.at[e]))
        copies[-1].start()
    for copy in copies:
        copy.wait()


def near_kernel(mine, keep_ref, one_ref, two_ref, own_ref, *parts):
    width = one_ref.shape[1]
    for k, part in enumerate((own_ref, *parts)):
        here = slice(k * mine, (k + 1) * mine)
        for side, ref in enumerate((one_ref, two_ref)):
            columns = slice(side * width, (side + 1) * width)
            part[:, columns] = (
                keep_ref[here, columns].astype(F32) + ref[here, :].astype(F32)
            ).astype(part.dtype)


def hbm_specs(count):
    return [pl.BlockSpec(memory_space=pltpu.HBM)] * count


def vmem_specs(count):
    return [pl.BlockSpec(memory_space=pltpu.VMEM)] * count


def shards(
    tokens, routes, positions, combine_weights, cotangent, gate_weight, up_weight, down_weight
):
    experts, width, hidden = gate_weight.shape
    replicas = lax.axis_size("dp")
    groups = lax.axis_size("expert")
    tensor = lax.axis_size("tensor")
    group_size, top = routes.shape
    capacity = group_size // 2
    slots = experts * groups * capacity
    mine = tokens.shape[0]
    devices = groups * tensor
    rows = mine * devices
    both = ("expert", "tensor")

    def swap(values, distance):
        return lax.ppermute(values, both, [(i, i ^ distance) for i in range(devices)])

    weights = [
        pltpu.with_memory_space_constraint(jnp.swapaxes(w, 1, 2), pltpu.HBM)
        for w in (gate_weight, up_weight, down_weight)
    ]
    held = pltpu.VMEM((experts, hidden, width), BF16)
    ready = min(EARLY, experts)
    inputs = [
        pltpu.with_memory_space_constraint(x, pltpu.HBM)
        for x in (tokens, cotangent, routes.T, positions.T, combine_weights.T)
    ]
    row = jax.ShapeDtypeStruct((mine, 2 * width + LANES), BF16)
    sent = pl.pallas_call(
        pack_kernel,
        out_shape=row,
        in_specs=hbm_specs(5),
        out_specs=vmem_specs(1)[0],
        scratch_shapes=[
            pltpu.VMEM((top, group_size), jnp.int32),
            pltpu.VMEM((top, group_size), jnp.int32),
            pltpu.VMEM((top, group_size), F32),
            pltpu.SemaphoreType.DMA((5,)),
        ],
        compiler_params=pltpu.CompilerParams(vmem_limit_bytes=2 * 2**20),
        name="pack",
    )(*inputs)
    held_weights = pl.pallas_call(
        functools.partial(fetch_kernel, ready),
        out_shape=[held] * 2,
        in_specs=hbm_specs(2),
        out_specs=vmem_specs(2),
        scratch_shapes=[pltpu.SemaphoreType.DMA((experts, 2))],
        compiler_params=pltpu.CompilerParams(vmem_limit_bytes=2**20),
        name="fetch",
    )(*weights[:2])
    blocks = devices // 2
    kept = [pltpu.with_memory_space_constraint(w, pltpu.VMEM) for w in held_weights]
    near_rows, *held_weights = pl.pallas_call(
        join_kernel,
        out_shape=[jax.ShapeDtypeStruct((rows // 2, 2 * width + LANES), BF16)] + [held] * 2,
        in_specs=vmem_specs(blocks + 2),
        out_specs=vmem_specs(3),
        input_output_aliases={blocks: 1, blocks + 1: 2},
        compiler_params=pltpu.CompilerParams(vmem_limit_bytes=2 * 2**20),
        name="join",
    )(sent, *[swap(sent, 2 * k) for k in range(1, blocks)], *kept)
    far_rows = swap(near_rows, 1)

    pack_rows = slots // LANES * hidden + (width // replicas // LANES + 1) * rows
    half = jax.ShapeDtypeStruct((rows // 2, 2 * width), BF16)
    pack = jax.ShapeDtypeStruct((pack_rows, LANES), BF16)
    kept = [pltpu.with_memory_space_constraint(w, pltpu.VMEM) for w in held_weights]
    lead = min(LEAD, experts)
    slot_wide = jax.ShapeDtypeStruct((slots, width), BF16)
    slot_narrow = jax.ShapeDtypeStruct((slots, hidden), F32)
    outs = pl.pallas_call(
        functools.partial(
            activations_kernel, (top, capacity, groups, tensor, replicas), ready, lead
        ),
        out_shape=[held] * 3
        + [
            jax.ShapeDtypeStruct((slots, hidden), BF16),
            slot_narrow,
            slot_narrow,
            slot_wide,
            jax.ShapeDtypeStruct((rows, slots), BF16),
            jax.ShapeDtypeStruct((slots, 1), F32),
        ]
        + [pack] * replicas,
        in_specs=vmem_specs(2) + hbm_specs(3) + vmem_specs(2),
        out_specs=vmem_specs(9 + replicas),
        scratch_shapes=[
            pltpu.VMEM((slots, width), BF16),
            pltpu.SemaphoreType.DMA((experts, 2)),
            pltpu.SemaphoreType.DMA((experts, 1)),
        ],
        input_output_aliases={5: 0, 6: 1},
        compiler_params=pltpu.CompilerParams(vmem_limit_bytes=6 * 2**20),
        cost_estimate=pl.CostEstimate(
            flops=4 * slots * hidden * width,
            bytes_accessed=4 * experts * hidden * width,
            transcendentals=slots * hidden,
        ),
        name="activations",
    )(near_rows, far_rows, *weights, *kept)
    kept = [pltpu.with_memory_space_constraint(w, pltpu.VMEM) for w in outs[:3]]
    packs = outs[9:]
    side = jax.ShapeDtypeStruct((rows // 2, width), BF16)
    keep, send_one, send_two, _ = pl.pallas_call(
        functools.partial(outputs_kernel, lead),
        out_shape=[half, side, side, held],
        in_specs=vmem_specs(9) + hbm_specs(1),
        out_specs=vmem_specs(4),
        scratch_shapes=[
            pltpu.VMEM((slots, 2 * width), BF16),
            pltpu.VMEM((2, slots, hidden), BF16),
            pltpu.VMEM((TURNED, width, hidden), BF16),
            pltpu.SemaphoreType.DMA((experts, 1)),
        ],
        input_output_aliases={8: 3},
        compiler_params=pltpu.CompilerParams(vmem_limit_bytes=6 * 2**20),
        cost_estimate=pl.CostEstimate(
            flops=8 * slots * hidden * width,
            bytes_accessed=6 * experts * hidden * width,
            transcendentals=0,
        ),
        name="outputs",
    )(*outs[3:9], *kept, weights[2])

    own, *others_near = pl.pallas_call(
        functools.partial(near_kernel, mine),
        out_shape=[jax.ShapeDtypeStruct((mine, 2 * width), F32)]
        + [jax.ShapeDtypeStruct((mine, 2 * width), BF16)] * (devices // 2 - 1),
        in_specs=vmem_specs(3),
        out_specs=vmem_specs(devices // 2),
        compiler_params=pltpu.CompilerParams(vmem_limit_bytes=2 * 2**20),
        name="near",
    )(keep, swap(send_one, 1), swap(send_two, 1))
    received = [swap(part, 2 * k) for k, part in enumerate(others_near, 1)]

    arrived = [packs[0]]
    for k in range(1, replicas):
        arrived.append(lax.ppermute(packs[k], "dp", [(i, i ^ k) for i in range(replicas)]))
    share = width // replicas
    grad, total = pl.pallas_call(
        functools.partial(grad_kernel, (top, capacity, groups, tensor, replicas)),
        out_shape=[
            jax.ShapeDtypeStruct((experts, hidden, share), BF16),
            jax.ShapeDtypeStruct((mine, 2 * width), F32),
        ],
        in_specs=vmem_specs(replicas + 1),
        out_specs=[pl.BlockSpec(memory_space=pl.ANY)] + vmem_specs(1),
        scratch_shapes=[
            pltpu.VMEM((replicas * slots, share), BF16),
            pltpu.VMEM((hidden, replicas * slots), BF16),
            pltpu.VMEM((experts, hidden, share), BF16),
            pltpu.SemaphoreType.DMA((experts,)),
        ],
        compiler_params=pltpu.CompilerParams(vmem_limit_bytes=10 * 2**20),
        cost_estimate=pl.CostEstimate(
            flops=2 * replicas * slots * share * hidden,
            bytes_accessed=2 * experts * share * hidden,
            transcendentals=0,
        ),
        name="grad_down",
    )(*arrived, own)
    total = (total + sum(part.astype(F32) for part in received[::-1])).astype(BF16)
    return (total[:, :width], total[:, width:], jnp.swapaxes(grad, 1, 2))


def solution(mesh):
    return jax.shard_map(
        shards,
        mesh=mesh,
        in_specs=(
            P(("dp", "expert", "tensor"), None),
            P(("dp", "expert"), None),
            P(("dp", "expert"), None),
            P(("dp", "expert"), None),
            P(("dp", "expert", "tensor"), None),
            P("expert", None, "tensor"),
            P("expert", None, "tensor"),
            P("expert", None, "tensor"),
        ),
        out_specs=(
            P(("dp", "expert", "tensor"), None),
            P(("dp", "expert", "tensor"), None),
            P("expert", "dp", "tensor"),
        ),
        check_vma=False,
    )
```

```python
import functools

import jax
import jax.numpy as jnp
from jax import lax
from jax.experimental import pallas as pl
from jax.experimental.pallas import tpu as pltpu
from jax.sharding import PartitionSpec as P

F32 = jnp.float32
BF16 = jnp.bfloat16
LANES = 128
EARLY = 3
TURNED = 2
LEAD = 4
NT = (((1,), (1,)), ((), ()))
TN = (((0,), (0,)), ((), ()))


def whole_part(values, divisor):
    return jnp.floor((values + 0.5) * (1.0 / divisor))


def fiota(shape, axis):
    return lax.broadcasted_iota(jnp.int32, shape, axis).astype(F32)


def row_tokens(rows, devices, tensor):
    device = lax.axis_index("expert") * tensor + lax.axis_index("tensor")
    pair = lax.div(device, 2)
    parity = device - pair * 2
    mine = rows // devices
    row = lax.broadcasted_iota(jnp.int32, (rows, 1), 0)
    second = jnp.where(row >= rows // 2, 1, 0)
    within = row - second * (rows // 2)
    block = lax.div(within, jnp.full_like(within, mine))
    token = (block ^ pair) * (2 * mine) + (second ^ parity) * mine + within - block * mine
    return token.astype(F32)


def slot_tables(routing, token, top, first_expert, capacity, groups, slots):
    rows = routing.shape[0]
    lane = fiota((rows, slots), 1)
    expert = whole_part(lane, groups * capacity)
    inner = lane - expert * (groups * capacity)
    group = whole_part(inner, capacity)
    target = (expert + first_expert) * capacity + inner - group * capacity
    target = jnp.where(whole_part(token, rows // groups) == group, target, -1.0)
    names = routing[:, :top] * float(capacity) + routing[:, top : 2 * top]
    weights = routing[:, 2 * top : 3 * top] + routing[:, 3 * top : 4 * top]
    chosen = jnp.zeros((rows, slots), F32)
    gains = jnp.zeros((rows, slots), F32)
    for k in range(top):
        match = names[:, k : k + 1] == target
        chosen = chosen + jnp.where(match, 1.0, 0.0)
        gains = gains + jnp.where(match, weights[:, k : k + 1], 0.0)
    return chosen, gains


def column_blocks(width):
    return [(at, min(LANES, width - at)) for at in range(0, width, LANES)]


def fetch_experts(weights, held, sems, first, last):
    return [
        pltpu.make_async_copy(source.at[e], target.at[e], sems.at[e, i])
        for e in range(first, last)
        for i, (source, target) in enumerate(zip(weights, held))
    ]


def turn_block(source, target, part, parts):
    size = source.shape[1] // parts
    for at in range(part * size, (part + 1) * size, LANES):
        target[at : at + LANES, :] = source[:, at : at + LANES].T


def pack_kernel(*refs):
    sources, out_ref, targets, sems = refs[:5], refs[5], refs[6:11], refs[11]
    tokens_ref, cotangent_ref, routes_ref, positions_ref, weights_ref = targets
    mine, width = tokens_ref.shape
    top, group_size = routes_ref.shape
    copies = [
        pltpu.make_async_copy(source, target, sems.at[i])
        for i, (source, target) in enumerate(zip(sources, targets))
    ]
    for copy in copies:
        copy.start()
    for copy in copies:
        copy.wait()
    weights = weights_ref[...]
    high = weights.astype(BF16)
    low = (weights - high.astype(F32)).astype(BF16)
    table = jnp.concatenate(
        [routes_ref[...].astype(F32), positions_ref[...].astype(F32), high.astype(F32), low.astype(F32)],
        axis=0,
    ).astype(BF16)
    first = lax.axis_index("tensor") * mine
    column = lax.broadcasted_iota(jnp.int32, (mine, group_size), 1)
    row = lax.broadcasted_iota(jnp.int32, (mine, group_size), 0)
    pick = jnp.where(column == row + first, 1.0, 0.0).astype(BF16)
    routing = lax.dot_general(pick, table, NT, preferred_element_type=F32)
    out_ref[:, :width] = tokens_ref[...]
    out_ref[:, width : 2 * width] = cotangent_ref[...]
    out_ref[:, 2 * width :] = jnp.concatenate(
        [routing, jnp.zeros((mine, LANES - 4 * top), F32)], axis=1
    ).astype(BF16)


def join_kernel(*refs):
    out_ref = refs[-3]
    mine = refs[0].shape[0]
    for k, block in enumerate(refs[:-5]):
        out_ref[k * mine : (k + 1) * mine, :] = block[...]


def fetch_kernel(last, *refs):
    weights, held, sems = refs[:2], refs[2:4], refs[4]
    copies = fetch_experts(weights, held, sems, 0, last)
    for copy in copies:
        copy.start()
    for copy in copies:
        copy.wait()


def activations_kernel(
    sizes, ready, lead, x_ref, far_ref, gate_hbm, up_hbm, down_hbm, *rest
):
    top, capacity, groups, tensor, replicas = sizes
    gate_w, up_w, down_w, activations, slope_ref, swish_ref, grads_ref, picker_ref, gain_ref = rest[2:11]
    packs = rest[11 : 11 + replicas]
    filled, sems, down_sems = rest[11 + replicas :]
    experts, hidden, width = gate_hbm.shape
    half = x_ref.shape[0]
    rows = 2 * half
    slots = filled.shape[0]
    per_expert = slots // experts
    batches = [
        fetch_experts((gate_hbm, up_hbm), (gate_w, up_w), sems, first, min(first + 2, experts))
        for first in range(ready, experts, 2)
    ]
    downs = fetch_experts((down_hbm,), (down_w,), down_sems, 0, lead)
    for copy in sum(batches[:2], []) + (downs if len(batches) < 3 else []):
        copy.start()

    first_expert = (lax.axis_index("expert") * experts).astype(F32)
    routing = jnp.concatenate([x_ref[:, 2 * width :], far_ref[:, 2 * width :]], axis=0).astype(F32)
    token = row_tokens(rows, groups * tensor, tensor)
    chosen, gains = slot_tables(routing, token, top, first_expert, capacity, groups, slots)
    scatter = chosen.T.astype(BF16)
    gain = jnp.sum(gains.T, axis=1, keepdims=True)
    gain_ref[...] = gain
    picker_ref[...] = chosen.astype(BF16)
    step = min(512, width)
    def fill(at):
        given = jnp.concatenate([x_ref[:, at : at + step], far_ref[:, at : at + step]], axis=0)
        return jnp.dot(scatter, given, preferred_element_type=F32)

    def fill_grads(at):
        grads_ref[:, at : at + step] = (gain * fill(width + at)).astype(BF16)

    for at in range(0, width, step):
        filled[:, at : at + step] = fill(at).astype(BF16)
    unfilled = list(range(0, width, step))

    for e in range(experts):
        if e >= ready and (e - ready) % 2 == 0:
            at = (e - ready) // 2
            for column in unfilled[:2]:
                fill_grads(column)
            unfilled = unfilled[2:]
            for copy in batches[at]:
                copy.wait()
            for copy in batches[at + 2] if at + 2 < len(batches) else []:
                copy.start()
            if at + 3 == len(batches):
                for copy in downs:
                    copy.start()
        here = slice(e * per_expert, (e + 1) * per_expert)
        slot_rows = filled[here, :]
        gate_pre = lax.dot_general(slot_rows, gate_w[e], NT, preferred_element_type=F32)
        up_pre = lax.dot_general(slot_rows, up_w[e], NT, preferred_element_type=F32)
        squash = 1.0 / (1.0 + jnp.exp(-gate_pre))
        swish = gate_pre * squash
        activations[here, :] = (swish * up_pre).astype(BF16)
        slope_ref[here, :] = up_pre * squash * (1.0 + gate_pre * (1.0 - squash))
        swish_ref[here, :] = swish
    replica = lax.axis_index("dp")
    share = width // replicas
    turned = {
        (block, lane): activations[block : block + LANES, lane : lane + size].T
        for block in range(0, slots, LANES)
        for lane, size in column_blocks(hidden)
    }
    for k in range(replicas):
        peer = replica ^ k
        at = 0
        for block in range(0, slots, LANES):
            for lane, size in column_blocks(hidden):
                packs[k][at : at + size, :] = turned[block, lane]
                at += size
        for lane in range(0, share, LANES):
            column = pl.multiple_of(width + peer * share + lane, LANES)
            packs[k][at : at + half, :] = x_ref[:, pl.ds(column, LANES)]
            packs[k][at + half : at + rows, :] = far_ref[:, pl.ds(column, LANES)]
            at += rows
        packs[k][at : at + half, :] = x_ref[:, 2 * width :]
        packs[k][at + half : at + rows, :] = far_ref[:, 2 * width :]
    for copy in downs:
        copy.wait()


def outputs_kernel(
    lead, activations, slope_ref, swish_ref, grads_ref, picker_ref, gain_ref, gate_w, up_w, unused, down_hbm,
    keep_ref, send_one, send_two, down_w, results, backs, turned, sems
):
    experts, _, width = gate_w.shape
    half = keep_ref.shape[0]
    slots = activations.shape[0]
    per_expert = slots // experts
    copies = fetch_experts((down_hbm,), (down_w,), sems, lead, experts)
    for copy in copies:
        copy.start()
    def arrive(e):
        if e >= lead and (e - lead) % 2 == 0:
            for copy in copies[e - lead : e - lead + 2]:
                copy.wait()

    def turn(e, part):
        if e < experts:
            turn_block(down_w.at[e], turned.at[e % TURNED], part, 4)

    def place(e):
        return slice(e * per_expert, (e + 1) * per_expert)

    arrive(0)
    for e in range(experts + 1):
        arrive(e + 1)
        turn(e + 1, 0)
        if e < experts:
            here = place(e)
            if e > 0:
                act_grad = jnp.dot(grads_ref[here, :], turned[e % TURNED], preferred_element_type=F32)
            else:
                act_grad = lax.dot_general(
                    grads_ref[here, :], down_w[e], NT, preferred_element_type=F32
                )
            backs[0, here, :] = (act_grad * slope_ref[here, :]).astype(BF16)
            backs[1, here, :] = (act_grad * swish_ref[here, :]).astype(BF16)
        turn(e + 1, 1)
        if e < experts:
            forward = jnp.dot(activations[here, :], down_w[e], preferred_element_type=F32)
            results[here, :width] = (
                forward.astype(BF16).astype(F32) * gain_ref[here, :]
            ).astype(BF16)
        turn(e + 1, 2)
        if e > 0:
            there = place(e - 1)
            back = jnp.dot(backs[0, there, :], gate_w[e - 1], preferred_element_type=F32)
        turn(e + 1, 3)
        if e > 0:
            back = back + jnp.dot(backs[1, there, :], up_w[e - 1], preferred_element_type=F32)
            results[there, width:] = back.astype(BF16)

    step = min(512, width)
    for at in range(0, 2 * width, step):
        total = jnp.dot(picker_ref[...], results[:, at : at + step], preferred_element_type=F32)
        keep_ref[:, at : at + step] = total[:half].astype(BF16)
        send_ref = send_one if at < width else send_two
        to = at % width
        send_ref[:, to : to + step] = total[half:].astype(BF16)


def grad_kernel(sizes, *refs):
    top, capacity, groups, tensor, replicas = sizes
    packs = refs[:replicas]
    own_ref, out_hbm, own_out, grads, acts, result, sems = refs[replicas:]
    experts, hidden, share = out_hbm.shape
    per_replica = groups * capacity
    slots = experts * per_replica
    per_expert = replicas * per_replica
    act_rows = slots // LANES * hidden
    rows = (packs[0].shape[0] - act_rows) // (share // LANES + 1)

    first_expert = (lax.axis_index("expert") * experts).astype(F32)
    token = row_tokens(rows, groups * tensor, tensor)
    for k in range(replicas):
        at = act_rows
        routing = packs[k][at + (share // LANES) * rows :, :].astype(F32)
        chosen, gains = slot_tables(
            routing, token, top, first_expert, capacity, groups, slots
        )
        scatter = chosen.T.astype(BF16)
        gain = jnp.sum(gains.T, axis=1, keepdims=True)
        for lane in range(0, share, LANES):
            filled = jnp.dot(scatter, packs[k][at : at + rows, :], preferred_element_type=F32)
            filled = (gain * filled).astype(BF16)
            for e in range(experts):
                to = e * per_expert + k * per_replica
                grads[to : to + per_replica, lane : lane + LANES] = filled[
                    e * per_replica : (e + 1) * per_replica
                ]
            at += rows

    left = jnp.concatenate(
        [
            packs[k][block * hidden : (block + 1) * hidden, :]
            for k in range(replicas)
            for block in range(slots // LANES)
        ],
        axis=1,
    )
    if experts > 1:
        lanes = replicas * slots
        before = fiota((lanes, lanes), 0)
        after = fiota((lanes, lanes), 1)
        source = whole_part(before, slots)
        inner = before - source * slots
        expert = whole_part(inner, per_replica)
        place = expert * per_expert + source * per_replica + inner - expert * per_replica
        order = jnp.where(place == after, 1.0, 0.0).astype(BF16)
        left = jnp.dot(left, order, preferred_element_type=F32).astype(BF16)
    acts[...] = left

    own_out[...] = own_ref[...].astype(F32)

    copies = []
    for e in range(experts):
        low = e * per_expert // LANES * LANES
        high = -(-(e + 1) * per_expert // LANES) * LANES
        right = grads[low:high, :]
        if high - low > per_expert:
            row = lax.broadcasted_iota(jnp.int32, right.shape, 0) + low
            inside = (row >= e * per_expert) & (row < (e + 1) * per_expert)
            right = jnp.where(inside, right.astype(F32), 0.0).astype(BF16)
        total = jnp.dot(acts[:, low:high], right, preferred_element_type=F32)
        result[e] = (total * (1.0 / replicas)).astype(BF16)
        copies.append(pltpu.make_async_copy(result.at[e], out_hbm.at[e], sems.at[e]))
        copies[-1].start()
    for copy in copies:
        copy.wait()


def near_kernel(mine, keep_ref, one_ref, two_ref, own_ref, *parts):
    width = one_ref.shape[1]
    for k, part in enumerate((own_ref, *parts)):
        here = slice(k * mine, (k + 1) * mine)
        for side, ref in enumerate((one_ref, two_ref)):
            columns = slice(side * width, (side + 1) * width)
            part[:, columns] = (
                keep_ref[here, columns].astype(F32) + ref[here, :].astype(F32)
            ).astype(part.dtype)


def hbm_specs(count):
    return [pl.BlockSpec(memory_space=pltpu.HBM)] * count


def vmem_specs(count):
    return [pl.BlockSpec(memory_space=pltpu.VMEM)] * count


def shards(
    tokens, routes, positions, combine_weights, cotangent, gate_weight, up_weight, down_weight
):
    experts, width, hidden = gate_weight.shape
    replicas = lax.axis_size("dp")
    groups = lax.axis_size("expert")
    tensor = lax.axis_size("tensor")
    group_size, top = routes.shape
    capacity = group_size // 2
    slots = experts * groups * capacity
    mine = tokens.shape[0]
    devices = groups * tensor
    rows = mine * devices
    both = ("expert", "tensor")

    def swap(values, distance):
        return lax.ppermute(values, both, [(i, i ^ distance) for i in range(devices)])

    weights = [
        pltpu.with_memory_space_constraint(jnp.swapaxes(w, 1, 2), pltpu.HBM)
        for w in (gate_weight, up_weight, down_weight)
    ]
    held = pltpu.VMEM((experts, hidden, width), BF16)
    ready = min(EARLY, experts)
    inputs = [
        pltpu.with_memory_space_constraint(x, pltpu.HBM)
        for x in (tokens, cotangent, routes.T, positions.T, combine_weights.T)
    ]
    row = jax.ShapeDtypeStruct((mine, 2 * width + LANES), BF16)
    sent = pl.pallas_call(
        pack_kernel,
        out_shape=row,
        in_specs=hbm_specs(5),
        out_specs=vmem_specs(1)[0],
        scratch_shapes=[
            pltpu.VMEM((mine, width), BF16),
            pltpu.VMEM((mine, width), BF16),
            pltpu.VMEM((top, group_size), jnp.int32),
            pltpu.VMEM((top, group_size), jnp.int32),
            pltpu.VMEM((top, group_size), F32),
            pltpu.SemaphoreType.DMA((5,)),
        ],
        compiler_params=pltpu.CompilerParams(vmem_limit_bytes=2 * 2**20),
        name="pack",
    )(*inputs)
    held_weights = pl.pallas_call(
        functools.partial(fetch_kernel, ready),
        out_shape=[held] * 2,
        in_specs=hbm_specs(2),
        out_specs=vmem_specs(2),
        scratch_shapes=[pltpu.SemaphoreType.DMA((experts, 2))],
        compiler_params=pltpu.CompilerParams(vmem_limit_bytes=2**20),
        name="fetch",
    )(*weights[:2])
    blocks = devices // 2
    kept = [pltpu.with_memory_space_constraint(w, pltpu.VMEM) for w in held_weights]
    near_rows, *held_weights = pl.pallas_call(
        join_kernel,
        out_shape=[jax.ShapeDtypeStruct((rows // 2, 2 * width + LANES), BF16)] + [held] * 2,
        in_specs=vmem_specs(blocks + 2),
        out_specs=vmem_specs(3),
        input_output_aliases={blocks: 1, blocks + 1: 2},
        compiler_params=pltpu.CompilerParams(vmem_limit_bytes=2 * 2**20),
        name="join",
    )(sent, *[swap(sent, 2 * k) for k in range(1, blocks)], *kept)
    far_rows = swap(near_rows, 1)

    pack_rows = slots // LANES * hidden + (width // replicas // LANES + 1) * rows
    half = jax.ShapeDtypeStruct((rows // 2, 2 * width), BF16)
    pack = jax.ShapeDtypeStruct((pack_rows, LANES), BF16)
    kept = [pltpu.with_memory_space_constraint(w, pltpu.VMEM) for w in held_weights]
    lead = min(LEAD, experts)
    slot_wide = jax.ShapeDtypeStruct((slots, width), BF16)
    slot_narrow = jax.ShapeDtypeStruct((slots, hidden), F32)
    outs = pl.pallas_call(
        functools.partial(
            activations_kernel, (top, capacity, groups, tensor, replicas), ready, lead
        ),
        out_shape=[held] * 3
        + [
            jax.ShapeDtypeStruct((slots, hidden), BF16),
            slot_narrow,
            slot_narrow,
            slot_wide,
            jax.ShapeDtypeStruct((rows, slots), BF16),
            jax.ShapeDtypeStruct((slots, 1), F32),
        ]
        + [pack] * replicas,
        in_specs=vmem_specs(2) + hbm_specs(3) + vmem_specs(2),
        out_specs=vmem_specs(9 + replicas),
        scratch_shapes=[
            pltpu.VMEM((slots, width), BF16),
            pltpu.SemaphoreType.DMA((experts, 2)),
            pltpu.SemaphoreType.DMA((experts, 1)),
        ],
        input_output_aliases={5: 0, 6: 1},
        compiler_params=pltpu.CompilerParams(vmem_limit_bytes=6 * 2**20),
        cost_estimate=pl.CostEstimate(
            flops=4 * slots * hidden * width,
            bytes_accessed=4 * experts * hidden * width,
            transcendentals=slots * hidden,
        ),
        name="activations",
    )(near_rows, far_rows, *weights, *kept)
    kept = [pltpu.with_memory_space_constraint(w, pltpu.VMEM) for w in outs[:3]]
    packs = outs[9:]
    side = jax.ShapeDtypeStruct((rows // 2, width), BF16)
    keep, send_one, send_two, _ = pl.pallas_call(
        functools.partial(outputs_kernel, lead),
        out_shape=[half, side, side, held],
        in_specs=vmem_specs(9) + hbm_specs(1),
        out_specs=vmem_specs(4),
        scratch_shapes=[
            pltpu.VMEM((slots, 2 * width), BF16),
            pltpu.VMEM((2, slots, hidden), BF16),
            pltpu.VMEM((TURNED, width, hidden), BF16),
            pltpu.SemaphoreType.DMA((experts, 1)),
        ],
        input_output_aliases={8: 3},
        compiler_params=pltpu.CompilerParams(vmem_limit_bytes=6 * 2**20),
        cost_estimate=pl.CostEstimate(
            flops=8 * slots * hidden * width,
            bytes_accessed=6 * experts * hidden * width,
            transcendentals=0,
        ),
        name="outputs",
    )(*outs[3:9], *kept, weights[2])

    own, *others_near = pl.pallas_call(
        functools.partial(near_kernel, mine),
        out_shape=[jax.ShapeDtypeStruct((mine, 2 * width), F32)]
        + [jax.ShapeDtypeStruct((mine, 2 * width), BF16)] * (devices // 2 - 1),
        in_specs=vmem_specs(3),
        out_specs=vmem_specs(devices // 2),
        compiler_params=pltpu.CompilerParams(vmem_limit_bytes=2 * 2**20),
        name="near",
    )(keep, swap(send_one, 1), swap(send_two, 1))
    received = [swap(part, 2 * k) for k, part in enumerate(others_near, 1)]

    arrived = [packs[0]]
    for k in range(1, replicas):
        arrived.append(lax.ppermute(packs[k], "dp", [(i, i ^ k) for i in range(replicas)]))
    share = width // replicas
    grad, total = pl.pallas_call(
        functools.partial(grad_kernel, (top, capacity, groups, tensor, replicas)),
        out_shape=[
            jax.ShapeDtypeStruct((experts, hidden, share), BF16),
            jax.ShapeDtypeStruct((mine, 2 * width), F32),
        ],
        in_specs=vmem_specs(replicas + 1),
        out_specs=[pl.BlockSpec(memory_space=pl.ANY)] + vmem_specs(1),
        scratch_shapes=[
            pltpu.VMEM((replicas * slots, share), BF16),
            pltpu.VMEM((hidden, replicas * slots), BF16),
            pltpu.VMEM((experts, hidden, share), BF16),
            pltpu.SemaphoreType.DMA((experts,)),
        ],
        compiler_params=pltpu.CompilerParams(vmem_limit_bytes=10 * 2**20),
        cost_estimate=pl.CostEstimate(
            flops=2 * replicas * slots * share * hidden,
            bytes_accessed=2 * experts * share * hidden,
            transcendentals=0,
        ),
        name="grad_down",
    )(*arrived, own)
    total = (total + sum(part.astype(F32) for part in received[::-1])).astype(BF16)
    return (total[:, :width], total[:, width:], jnp.swapaxes(grad, 1, 2))


def solution(mesh):
    return jax.shard_map(
        shards,
        mesh=mesh,
        in_specs=(
            P(("dp", "expert", "tensor"), None),
            P(("dp", "expert"), None),
            P(("dp", "expert"), None),
            P(("dp", "expert"), None),
            P(("dp", "expert", "tensor"), None),
            P("expert", None, "tensor"),
            P("expert", None, "tensor"),
            P("expert", None, "tensor"),
        ),
        out_specs=(
            P(("dp", "expert", "tensor"), None),
            P(("dp", "expert", "tensor"), None),
            P("expert", "dp", "tensor"),
        ),
        check_vma=False,
    )
```

```python
import functools

import jax
import jax.numpy as jnp
from jax import lax
from jax.experimental import pallas as pl
from jax.experimental.pallas import tpu as pltpu
from jax.sharding import PartitionSpec as P

F32 = jnp.float32
BF16 = jnp.bfloat16
LANES = 128
EARLY = 3
TURNED = 2
LEAD = 4
NT = (((1,), (1,)), ((), ()))
TN = (((0,), (0,)), ((), ()))


def whole_part(values, divisor):
    return jnp.floor((values + 0.5) * (1.0 / divisor))


def fiota(shape, axis):
    return lax.broadcasted_iota(jnp.int32, shape, axis).astype(F32)


def row_tokens(rows, devices, tensor):
    device = lax.axis_index("expert") * tensor + lax.axis_index("tensor")
    pair = lax.div(device, 2)
    parity = device - pair * 2
    mine = rows // devices
    row = lax.broadcasted_iota(jnp.int32, (rows, 1), 0)
    second = jnp.where(row >= rows // 2, 1, 0)
    within = row - second * (rows // 2)
    block = lax.div(within, jnp.full_like(within, mine))
    token = (block ^ pair) * (2 * mine) + (second ^ parity) * mine + within - block * mine
    return token.astype(F32)


def slot_tables(routing, token, top, first_expert, capacity, groups, slots):
    rows = routing.shape[0]
    lane = fiota((rows, slots), 1)
    expert = whole_part(lane, groups * capacity)
    inner = lane - expert * (groups * capacity)
    group = whole_part(inner, capacity)
    target = (expert + first_expert) * capacity + inner - group * capacity
    target = jnp.where(whole_part(token, rows // groups) == group, target, -1.0)
    names = routing[:, :top] * float(capacity) + routing[:, top : 2 * top]
    weights = routing[:, 2 * top : 3 * top] + routing[:, 3 * top : 4 * top]
    chosen = jnp.zeros((rows, slots), F32)
    gains = jnp.zeros((rows, slots), F32)
    for k in range(top):
        match = names[:, k : k + 1] == target
        chosen = chosen + jnp.where(match, 1.0, 0.0)
        gains = gains + jnp.where(match, weights[:, k : k + 1], 0.0)
    return chosen, gains


def column_blocks(width):
    return [(at, min(LANES, width - at)) for at in range(0, width, LANES)]


def fetch_experts(weights, held, sems, first, last):
    return [
        pltpu.make_async_copy(source.at[e], target.at[e], sems.at[e, i])
        for e in range(first, last)
        for i, (source, target) in enumerate(zip(weights, held))
    ]


def turn_block(source, target, part, parts):
    size = source.shape[1] // parts
    for at in range(part * size, (part + 1) * size, LANES):
        target[at : at + LANES, :] = source[:, at : at + LANES].T


def pack_kernel(*refs):
    sources, out_ref, targets, sems = refs[:5], refs[5], refs[6:11], refs[11]
    tokens_ref, cotangent_ref, routes_ref, positions_ref, weights_ref = targets
    mine, width = tokens_ref.shape
    top, group_size = routes_ref.shape
    copies = [
        pltpu.make_async_copy(source, target, sems.at[i])
        for i, (source, target) in enumerate(zip(sources, targets))
    ]
    for copy in copies[2:] + copies[:2]:
        copy.start()
    for copy in copies[2:]:
        copy.wait()
    weights = weights_ref[...]
    high = weights.astype(BF16)
    low = (weights - high.astype(F32)).astype(BF16)
    table = jnp.concatenate(
        [routes_ref[...].astype(F32), positions_ref[...].astype(F32), high.astype(F32), low.astype(F32)],
        axis=0,
    ).astype(BF16)
    first = lax.axis_index("tensor") * mine
    column = lax.broadcasted_iota(jnp.int32, (mine, group_size), 1)
    row = lax.broadcasted_iota(jnp.int32, (mine, group_size), 0)
    pick = jnp.where(column == row + first, 1.0, 0.0).astype(BF16)
    routing = lax.dot_general(pick, table, NT, preferred_element_type=F32)
    out_ref[:, 2 * width :] = jnp.concatenate(
        [routing, jnp.zeros((mine, LANES - 4 * top), F32)], axis=1
    ).astype(BF16)
    for copy in copies[:2]:
        copy.wait()
    out_ref[:, :width] = tokens_ref[...]
    out_ref[:, width : 2 * width] = cotangent_ref[...]


def join_kernel(*refs):
    out_ref = refs[-3]
    mine = refs[0].shape[0]
    for k, block in enumerate(refs[:-5]):
        out_ref[k * mine : (k + 1) * mine, :] = block[...]


def fetch_kernel(last, *refs):
    weights, held, sems = refs[:2], refs[2:4], refs[4]
    copies = fetch_experts(weights, held, sems, 0, last)
    for copy in copies:
        copy.start()
    for copy in copies:
        copy.wait()


def activations_kernel(
    sizes, ready, lead, x_ref, far_ref, gate_hbm, up_hbm, down_hbm, *rest
):
    top, capacity, groups, tensor, replicas = sizes
    gate_w, up_w, down_w, activations, slope_ref, swish_ref, grads_ref, picker_ref, gain_ref = rest[2:11]
    packs = rest[11 : 11 + replicas]
    filled, sems, down_sems = rest[11 + replicas :]
    experts, hidden, width = gate_hbm.shape
    half = x_ref.shape[0]
    rows = 2 * half
    slots = filled.shape[0]
    per_expert = slots // experts
    batches = [
        fetch_experts((gate_hbm, up_hbm), (gate_w, up_w), sems, first, min(first + 2, experts))
        for first in range(ready, experts, 2)
    ]
    downs = fetch_experts((down_hbm,), (down_w,), down_sems, 0, lead)
    for copy in sum(batches[:2], []) + (downs if len(batches) < 3 else []):
        copy.start()

    first_expert = (lax.axis_index("expert") * experts).astype(F32)
    routing = jnp.concatenate([x_ref[:, 2 * width :], far_ref[:, 2 * width :]], axis=0).astype(F32)
    token = row_tokens(rows, groups * tensor, tensor)
    chosen, gains = slot_tables(routing, token, top, first_expert, capacity, groups, slots)
    scatter = chosen.T.astype(BF16)
    gain = jnp.sum(gains.T, axis=1, keepdims=True)
    gain_ref[...] = gain
    picker_ref[...] = chosen.astype(BF16)
    step = min(512, width)
    def fill(at):
        given = jnp.concatenate([x_ref[:, at : at + step], far_ref[:, at : at + step]], axis=0)
        return jnp.dot(scatter, given, preferred_element_type=F32)

    def fill_grads(at):
        grads_ref[:, at : at + step] = (gain * fill(width + at)).astype(BF16)

    for at in range(0, width, step):
        filled[:, at : at + step] = fill(at).astype(BF16)
    unfilled = list(range(0, width, step))

    for e in range(experts):
        if e >= ready and (e - ready) % 2 == 0:
            at = (e - ready) // 2
            for column in unfilled[:2]:
                fill_grads(column)
            unfilled = unfilled[2:]
            for copy in batches[at]:
                copy.wait()
            for copy in batches[at + 2] if at + 2 < len(batches) else []:
                copy.start()
            if at + 3 == len(batches):
                for copy in downs:
                    copy.start()
        here = slice(e * per_expert, (e + 1) * per_expert)
        slot_rows = filled[here, :]
        gate_pre = lax.dot_general(slot_rows, gate_w[e], NT, preferred_element_type=F32)
        up_pre = lax.dot_general(slot_rows, up_w[e], NT, preferred_element_type=F32)
        squash = 1.0 / (1.0 + jnp.exp(-gate_pre))
        swish = gate_pre * squash
        activations[here, :] = (swish * up_pre).astype(BF16)
        slope_ref[here, :] = up_pre * squash * (1.0 + gate_pre * (1.0 - squash))
        swish_ref[here, :] = swish
    replica = lax.axis_index("dp")
    share = width // replicas
    turned = {
        (block, lane): activations[block : block + LANES, lane : lane + size].T
        for block in range(0, slots, LANES)
        for lane, size in column_blocks(hidden)
    }
    for k in range(replicas):
        peer = replica ^ k
        at = 0
        for block in range(0, slots, LANES):
            for lane, size in column_blocks(hidden):
                packs[k][at : at + size, :] = turned[block, lane]
                at += size
        for lane in range(0, share, LANES):
            column = pl.multiple_of(width + peer * share + lane, LANES)
            packs[k][at : at + half, :] = x_ref[:, pl.ds(column, LANES)]
            packs[k][at + half : at + rows, :] = far_ref[:, pl.ds(column, LANES)]
            at += rows
        packs[k][at : at + half, :] = x_ref[:, 2 * width :]
        packs[k][at + half : at + rows, :] = far_ref[:, 2 * width :]
    for copy in downs:
        copy.wait()


def outputs_kernel(
    lead, activations, slope_ref, swish_ref, grads_ref, picker_ref, gain_ref, gate_w, up_w, unused, down_hbm,
    keep_ref, send_one, send_two, down_w, results, backs, turned, sems
):
    experts, _, width = gate_w.shape
    half = keep_ref.shape[0]
    slots = activations.shape[0]
    per_expert = slots // experts
    copies = fetch_experts((down_hbm,), (down_w,), sems, lead, experts)
    for copy in copies:
        copy.start()
    def arrive(e):
        if e >= lead and (e - lead) % 2 == 0:
            for copy in copies[e - lead : e - lead + 2]:
                copy.wait()

    def turn(e, part):
        if e < experts:
            turn_block(down_w.at[e], turned.at[e % TURNED], part, 4)

    def place(e):
        return slice(e * per_expert, (e + 1) * per_expert)

    arrive(0)
    for e in range(experts + 1):
        arrive(e + 1)
        turn(e + 1, 0)
        if e < experts:
            here = place(e)
            if e > 0:
                act_grad = jnp.dot(grads_ref[here, :], turned[e % TURNED], preferred_element_type=F32)
            else:
                act_grad = lax.dot_general(
                    grads_ref[here, :], down_w[e], NT, preferred_element_type=F32
                )
            backs[0, here, :] = (act_grad * slope_ref[here, :]).astype(BF16)
            backs[1, here, :] = (act_grad * swish_ref[here, :]).astype(BF16)
        turn(e + 1, 1)
        if e < experts:
            forward = jnp.dot(activations[here, :], down_w[e], preferred_element_type=F32)
            results[here, :width] = (
                forward.astype(BF16).astype(F32) * gain_ref[here, :]
            ).astype(BF16)
        turn(e + 1, 2)
        if e > 0:
            there = place(e - 1)
            back = jnp.dot(backs[0, there, :], gate_w[e - 1], preferred_element_type=F32)
        turn(e + 1, 3)
        if e > 0:
            back = back + jnp.dot(backs[1, there, :], up_w[e - 1], preferred_element_type=F32)
            results[there, width:] = back.astype(BF16)

    step = min(512, width)
    for at in range(0, 2 * width, step):
        total = jnp.dot(picker_ref[...], results[:, at : at + step], preferred_element_type=F32)
        keep_ref[:, at : at + step] = total[:half].astype(BF16)
        send_ref = send_one if at < width else send_two
        to = at % width
        send_ref[:, to : to + step] = total[half:].astype(BF16)


def grad_kernel(sizes, *refs):
    top, capacity, groups, tensor, replicas = sizes
    packs = refs[:replicas]
    own_ref, out_hbm, own_out, grads, acts, result, sems = refs[replicas:]
    experts, hidden, share = out_hbm.shape
    per_replica = groups * capacity
    slots = experts * per_replica
    per_expert = replicas * per_replica
    act_rows = slots // LANES * hidden
    rows = (packs[0].shape[0] - act_rows) // (share // LANES + 1)

    first_expert = (lax.axis_index("expert") * experts).astype(F32)
    token = row_tokens(rows, groups * tensor, tensor)
    for k in range(replicas):
        at = act_rows
        routing = packs[k][at + (share // LANES) * rows :, :].astype(F32)
        chosen, gains = slot_tables(
            routing, token, top, first_expert, capacity, groups, slots
        )
        scatter = chosen.T.astype(BF16)
        gain = jnp.sum(gains.T, axis=1, keepdims=True)
        for lane in range(0, share, LANES):
            filled = jnp.dot(scatter, packs[k][at : at + rows, :], preferred_element_type=F32)
            filled = (gain * filled).astype(BF16)
            for e in range(experts):
                to = e * per_expert + k * per_replica
                grads[to : to + per_replica, lane : lane + LANES] = filled[
                    e * per_replica : (e + 1) * per_replica
                ]
            at += rows

    left = jnp.concatenate(
        [
            packs[k][block * hidden : (block + 1) * hidden, :]
            for k in range(replicas)
            for block in range(slots // LANES)
        ],
        axis=1,
    )
    if experts > 1:
        lanes = replicas * slots
        before = fiota((lanes, lanes), 0)
        after = fiota((lanes, lanes), 1)
        source = whole_part(before, slots)
        inner = before - source * slots
        expert = whole_part(inner, per_replica)
        place = expert * per_expert + source * per_replica + inner - expert * per_replica
        order = jnp.where(place == after, 1.0, 0.0).astype(BF16)
        left = jnp.dot(left, order, preferred_element_type=F32).astype(BF16)
    acts[...] = left

    own_out[...] = own_ref[...].astype(F32)

    copies = []
    for e in range(experts):
        low = e * per_expert // LANES * LANES
        high = -(-(e + 1) * per_expert // LANES) * LANES
        right = grads[low:high, :]
        if high - low > per_expert:
            row = lax.broadcasted_iota(jnp.int32, right.shape, 0) + low
            inside = (row >= e * per_expert) & (row < (e + 1) * per_expert)
            right = jnp.where(inside, right.astype(F32), 0.0).astype(BF16)
        total = jnp.dot(acts[:, low:high], right, preferred_element_type=F32)
        result[e] = (total * (1.0 / replicas)).astype(BF16)
        copies.append(pltpu.make_async_copy(result.at[e], out_hbm.at[e], sems.at[e]))
        copies[-1].start()
    for copy in copies:
        copy.wait()


def near_kernel(mine, keep_ref, one_ref, two_ref, own_ref, *parts):
    width = one_ref.shape[1]
    for k, part in enumerate((own_ref, *parts)):
        here = slice(k * mine, (k + 1) * mine)
        for side, ref in enumerate((one_ref, two_ref)):
            columns = slice(side * width, (side + 1) * width)
            part[:, columns] = (
                keep_ref[here, columns].astype(F32) + ref[here, :].astype(F32)
            ).astype(part.dtype)


def hbm_specs(count):
    return [pl.BlockSpec(memory_space=pltpu.HBM)] * count


def vmem_specs(count):
    return [pl.BlockSpec(memory_space=pltpu.VMEM)] * count


def shards(
    tokens, routes, positions, combine_weights, cotangent, gate_weight, up_weight, down_weight
):
    experts, width, hidden = gate_weight.shape
    replicas = lax.axis_size("dp")
    groups = lax.axis_size("expert")
    tensor = lax.axis_size("tensor")
    group_size, top = routes.shape
    capacity = group_size // 2
    slots = experts * groups * capacity
    mine = tokens.shape[0]
    devices = groups * tensor
    rows = mine * devices
    both = ("expert", "tensor")

    def swap(values, distance):
        return lax.ppermute(values, both, [(i, i ^ distance) for i in range(devices)])

    weights = [
        pltpu.with_memory_space_constraint(jnp.swapaxes(w, 1, 2), pltpu.HBM)
        for w in (gate_weight, up_weight, down_weight)
    ]
    held = pltpu.VMEM((experts, hidden, width), BF16)
    ready = min(EARLY, experts)
    inputs = [
        pltpu.with_memory_space_constraint(x, pltpu.HBM)
        for x in (tokens, cotangent, routes.T, positions.T, combine_weights.T)
    ]
    row = jax.ShapeDtypeStruct((mine, 2 * width + LANES), BF16)
    sent = pl.pallas_call(
        pack_kernel,
        out_shape=row,
        in_specs=hbm_specs(5),
        out_specs=vmem_specs(1)[0],
        scratch_shapes=[
            pltpu.VMEM((mine, width), BF16),
            pltpu.VMEM((mine, width), BF16),
            pltpu.VMEM((top, group_size), jnp.int32),
            pltpu.VMEM((top, group_size), jnp.int32),
            pltpu.VMEM((top, group_size), F32),
            pltpu.SemaphoreType.DMA((5,)),
        ],
        compiler_params=pltpu.CompilerParams(vmem_limit_bytes=2 * 2**20),
        name="pack",
    )(*inputs)
    held_weights = pl.pallas_call(
        functools.partial(fetch_kernel, ready),
        out_shape=[held] * 2,
        in_specs=hbm_specs(2),
        out_specs=vmem_specs(2),
        scratch_shapes=[pltpu.SemaphoreType.DMA((experts, 2))],
        compiler_params=pltpu.CompilerParams(vmem_limit_bytes=2**20),
        name="fetch",
    )(*weights[:2])
    blocks = devices // 2
    kept = [pltpu.with_memory_space_constraint(w, pltpu.VMEM) for w in held_weights]
    near_rows, *held_weights = pl.pallas_call(
        join_kernel,
        out_shape=[jax.ShapeDtypeStruct((rows // 2, 2 * width + LANES), BF16)] + [held] * 2,
        in_specs=vmem_specs(blocks + 2),
        out_specs=vmem_specs(3),
        input_output_aliases={blocks: 1, blocks + 1: 2},
        compiler_params=pltpu.CompilerParams(vmem_limit_bytes=2 * 2**20),
        name="join",
    )(sent, *[swap(sent, 2 * k) for k in range(1, blocks)], *kept)
    far_rows = swap(near_rows, 1)

    pack_rows = slots // LANES * hidden + (width // replicas // LANES + 1) * rows
    half = jax.ShapeDtypeStruct((rows // 2, 2 * width), BF16)
    pack = jax.ShapeDtypeStruct((pack_rows, LANES), BF16)
    kept = [pltpu.with_memory_space_constraint(w, pltpu.VMEM) for w in held_weights]
    lead = min(LEAD, experts)
    slot_wide = jax.ShapeDtypeStruct((slots, width), BF16)
    slot_narrow = jax.ShapeDtypeStruct((slots, hidden), F32)
    outs = pl.pallas_call(
        functools.partial(
            activations_kernel, (top, capacity, groups, tensor, replicas), ready, lead
        ),
        out_shape=[held] * 3
        + [
            jax.ShapeDtypeStruct((slots, hidden), BF16),
            slot_narrow,
            slot_narrow,
            slot_wide,
            jax.ShapeDtypeStruct((rows, slots), BF16),
            jax.ShapeDtypeStruct((slots, 1), F32),
        ]
        + [pack] * replicas,
        in_specs=vmem_specs(2) + hbm_specs(3) + vmem_specs(2),
        out_specs=vmem_specs(9 + replicas),
        scratch_shapes=[
            pltpu.VMEM((slots, width), BF16),
            pltpu.SemaphoreType.DMA((experts, 2)),
            pltpu.SemaphoreType.DMA((experts, 1)),
        ],
        input_output_aliases={5: 0, 6: 1},
        compiler_params=pltpu.CompilerParams(vmem_limit_bytes=6 * 2**20),
        cost_estimate=pl.CostEstimate(
            flops=4 * slots * hidden * width,
            bytes_accessed=4 * experts * hidden * width,
            transcendentals=slots * hidden,
        ),
        name="activations",
    )(near_rows, far_rows, *weights, *kept)
    kept = [pltpu.with_memory_space_constraint(w, pltpu.VMEM) for w in outs[:3]]
    packs = outs[9:]
    side = jax.ShapeDtypeStruct((rows // 2, width), BF16)
    keep, send_one, send_two, _ = pl.pallas_call(
        functools.partial(outputs_kernel, lead),
        out_shape=[half, side, side, held],
        in_specs=vmem_specs(9) + hbm_specs(1),
        out_specs=vmem_specs(4),
        scratch_shapes=[
            pltpu.VMEM((slots, 2 * width), BF16),
            pltpu.VMEM((2, slots, hidden), BF16),
            pltpu.VMEM((TURNED, width, hidden), BF16),
            pltpu.SemaphoreType.DMA((experts, 1)),
        ],
        input_output_aliases={8: 3},
        compiler_params=pltpu.CompilerParams(vmem_limit_bytes=6 * 2**20),
        cost_estimate=pl.CostEstimate(
            flops=8 * slots * hidden * width,
            bytes_accessed=6 * experts * hidden * width,
            transcendentals=0,
        ),
        name="outputs",
    )(*outs[3:9], *kept, weights[2])

    own, *others_near = pl.pallas_call(
        functools.partial(near_kernel, mine),
        out_shape=[jax.ShapeDtypeStruct((mine, 2 * width), F32)]
        + [jax.ShapeDtypeStruct((mine, 2 * width), BF16)] * (devices // 2 - 1),
        in_specs=vmem_specs(3),
        out_specs=vmem_specs(devices // 2),
        compiler_params=pltpu.CompilerParams(vmem_limit_bytes=2 * 2**20),
        name="near",
    )(keep, swap(send_one, 1), swap(send_two, 1))
    received = [swap(part, 2 * k) for k, part in enumerate(others_near, 1)]

    arrived = [packs[0]]
    for k in [*range(2, replicas), 1]:
        arrived.append(lax.ppermute(packs[k], "dp", [(i, i ^ k) for i in range(replicas)]))
    share = width // replicas
    grad, total = pl.pallas_call(
        functools.partial(grad_kernel, (top, capacity, groups, tensor, replicas)),
        out_shape=[
            jax.ShapeDtypeStruct((experts, hidden, share), BF16),
            jax.ShapeDtypeStruct((mine, 2 * width), F32),
        ],
        in_specs=vmem_specs(replicas + 1),
        out_specs=[pl.BlockSpec(memory_space=pl.ANY)] + vmem_specs(1),
        scratch_shapes=[
            pltpu.VMEM((replicas * slots, share), BF16),
            pltpu.VMEM((hidden, replicas * slots), BF16),
            pltpu.VMEM((experts, hidden, share), BF16),
            pltpu.SemaphoreType.DMA((experts,)),
        ],
        compiler_params=pltpu.CompilerParams(vmem_limit_bytes=10 * 2**20),
        cost_estimate=pl.CostEstimate(
            flops=2 * replicas * slots * share * hidden,
            bytes_accessed=2 * experts * share * hidden,
            transcendentals=0,
        ),
        name="grad_down",
    )(*arrived, own)
    total = (total + sum(part.astype(F32) for part in received[::-1])).astype(BF16)
    return (total[:, :width], total[:, width:], jnp.swapaxes(grad, 1, 2))


def solution(mesh):
    return jax.shard_map(
        shards,
        mesh=mesh,
        in_specs=(
            P(("dp", "expert", "tensor"), None),
            P(("dp", "expert"), None),
            P(("dp", "expert"), None),
            P(("dp", "expert"), None),
            P(("dp", "expert", "tensor"), None),
            P("expert", None, "tensor"),
            P("expert", None, "tensor"),
            P("expert", None, "tensor"),
        ),
        out_specs=(
            P(("dp", "expert", "tensor"), None),
            P(("dp", "expert", "tensor"), None),
            P("expert", "dp", "tensor"),
        ),
        check_vma=False,
    )
```

```python
import functools

import jax
import jax.numpy as jnp
from jax import lax
from jax.experimental import pallas as pl
from jax.experimental.pallas import tpu as pltpu
from jax.sharding import PartitionSpec as P

F32 = jnp.float32
BF16 = jnp.bfloat16
LANES = 128
EARLY = 3
TURNED = 2
LEAD = 4
NT = (((1,), (1,)), ((), ()))
TN = (((0,), (0,)), ((), ()))


def whole_part(values, divisor):
    return jnp.floor((values + 0.5) * (1.0 / divisor))


def fiota(shape, axis):
    return lax.broadcasted_iota(jnp.int32, shape, axis).astype(F32)


def row_tokens(rows, devices, tensor):
    device = lax.axis_index("expert") * tensor + lax.axis_index("tensor")
    pair = lax.div(device, 2)
    parity = device - pair * 2
    mine = rows // devices
    row = lax.broadcasted_iota(jnp.int32, (rows, 1), 0)
    second = jnp.where(row >= rows // 2, 1, 0)
    within = row - second * (rows // 2)
    block = lax.div(within, jnp.full_like(within, mine))
    token = (block ^ pair) * (2 * mine) + (second ^ parity) * mine + within - block * mine
    return token.astype(F32)


def slot_tables(routing, token, top, first_expert, capacity, groups, slots):
    rows = routing.shape[0]
    lane = fiota((rows, slots), 1)
    expert = whole_part(lane, groups * capacity)
    inner = lane - expert * (groups * capacity)
    group = whole_part(inner, capacity)
    target = (expert + first_expert) * capacity + inner - group * capacity
    target = jnp.where(whole_part(token, rows // groups) == group, target, -1.0)
    names = routing[:, :top] * float(capacity) + routing[:, top : 2 * top]
    weights = routing[:, 2 * top : 3 * top] + routing[:, 3 * top : 4 * top]
    chosen = jnp.zeros((rows, slots), F32)
    gains = jnp.zeros((rows, slots), F32)
    for k in range(top):
        match = names[:, k : k + 1] == target
        chosen = chosen + jnp.where(match, 1.0, 0.0)
        gains = gains + jnp.where(match, weights[:, k : k + 1], 0.0)
    return chosen, gains


def column_blocks(width):
    return [(at, min(LANES, width - at)) for at in range(0, width, LANES)]


def fetch_experts(weights, held, sems, first, last):
    return [
        pltpu.make_async_copy(source.at[e], target.at[e], sems.at[e, i])
        for e in range(first, last)
        for i, (source, target) in enumerate(zip(weights, held))
    ]


def turn_block(source, target, part, parts):
    size = source.shape[1] // parts
    for at in range(part * size, (part + 1) * size, LANES):
        target[at : at + LANES, :] = source[:, at : at + LANES].T


def pack_kernel(*refs):
    sources, out_ref, targets, sems = refs[:5], refs[5], refs[6:11], refs[11]
    tokens_ref, cotangent_ref, routes_ref, positions_ref, weights_ref = targets
    mine, width = tokens_ref.shape
    top, group_size = routes_ref.shape
    copies = [
        pltpu.make_async_copy(source, target, sems.at[i])
        for i, (source, target) in enumerate(zip(sources, targets))
    ]
    for copy in copies[2:] + copies[:2]:
        copy.start()
    for copy in copies[2:]:
        copy.wait()
    weights = weights_ref[...]
    high = weights.astype(BF16)
    low = (weights - high.astype(F32)).astype(BF16)
    table = jnp.concatenate(
        [routes_ref[...].astype(F32), positions_ref[...].astype(F32), high.astype(F32), low.astype(F32)],
        axis=0,
    ).astype(BF16)
    first = lax.axis_index("tensor") * mine
    column = lax.broadcasted_iota(jnp.int32, (mine, group_size), 1)
    row = lax.broadcasted_iota(jnp.int32, (mine, group_size), 0)
    pick = jnp.where(column == row + first, 1.0, 0.0).astype(BF16)
    routing = lax.dot_general(pick, table, NT, preferred_element_type=F32)
    out_ref[:, 2 * width :] = jnp.concatenate(
        [routing, jnp.zeros((mine, LANES - 4 * top), F32)], axis=1
    ).astype(BF16)
    for copy in copies[:2]:
        copy.wait()
    out_ref[:, :width] = tokens_ref[...]
    out_ref[:, width : 2 * width] = cotangent_ref[...]


def join_kernel(*refs):
    out_ref = refs[-3]
    mine = refs[0].shape[0]
    for k, block in enumerate(refs[:-5]):
        out_ref[k * mine : (k + 1) * mine, :] = block[...]


def fetch_kernel(last, *refs):
    weights, held, sems = refs[:2], refs[2:4], refs[4]
    copies = fetch_experts(weights, held, sems, 0, last)
    for copy in copies:
        copy.start()
    for copy in copies:
        copy.wait()


def activations_kernel(
    sizes, ready, lead, x_ref, far_ref, gate_hbm, up_hbm, down_hbm, *rest
):
    top, capacity, groups, tensor, replicas = sizes
    gate_w, up_w, down_w, activations, slope_ref, swish_ref, grads_ref, picker_ref, gain_ref = rest[2:11]
    packs = rest[11 : 11 + replicas]
    filled, sems, down_sems = rest[11 + replicas :]
    experts, hidden, width = gate_hbm.shape
    half = x_ref.shape[0]
    rows = 2 * half
    slots = filled.shape[0]
    per_expert = slots // experts
    batches = [
        fetch_experts((gate_hbm, up_hbm), (gate_w, up_w), sems, first, min(first + 2, experts))
        for first in range(ready, experts, 2)
    ]
    downs = fetch_experts((down_hbm,), (down_w,), down_sems, 0, lead)
    for copy in sum(batches[:2], []) + (downs if len(batches) < 3 else []):
        copy.start()

    first_expert = (lax.axis_index("expert") * experts).astype(F32)
    routing = jnp.concatenate([x_ref[:, 2 * width :], far_ref[:, 2 * width :]], axis=0).astype(F32)
    token = row_tokens(rows, groups * tensor, tensor)
    chosen, gains = slot_tables(routing, token, top, first_expert, capacity, groups, slots)
    scatter = chosen.T.astype(BF16)
    gain = jnp.sum(gains.T, axis=1, keepdims=True)
    gain_ref[...] = gain
    picker_ref[...] = chosen.astype(BF16)
    step = min(512, width)
    def fill(at):
        given = jnp.concatenate([x_ref[:, at : at + step], far_ref[:, at : at + step]], axis=0)
        return jnp.dot(scatter, given, preferred_element_type=F32)

    def fill_grads(at):
        grads_ref[:, at : at + step] = (gain * fill(width + at)).astype(BF16)

    for at in range(0, width, step):
        filled[:, at : at + step] = fill(at).astype(BF16)
    unfilled = list(range(0, width, step))

    for e in range(experts):
        if e >= ready and (e - ready) % 2 == 0:
            at = (e - ready) // 2
            for column in unfilled[:2]:
                fill_grads(column)
            unfilled = unfilled[2:]
            for copy in batches[at]:
                copy.wait()
            for copy in batches[at + 2] if at + 2 < len(batches) else []:
                copy.start()
            if at + 3 == len(batches):
                for copy in downs:
                    copy.start()
        here = slice(e * per_expert, (e + 1) * per_expert)
        slot_rows = filled[here, :]
        gate_pre = lax.dot_general(slot_rows, gate_w[e], NT, preferred_element_type=F32)
        up_pre = lax.dot_general(slot_rows, up_w[e], NT, preferred_element_type=F32)
        squash = 1.0 / (1.0 + jnp.exp(-gate_pre))
        swish = gate_pre * squash
        activations[here, :] = (swish * up_pre).astype(BF16)
        slope_ref[here, :] = up_pre * squash * (1.0 + gate_pre * (1.0 - squash))
        swish_ref[here, :] = swish
    replica = lax.axis_index("dp")
    share = width // replicas
    turned = {
        (block, lane): activations[block : block + LANES, lane : lane + size].T
        for block in range(0, slots, LANES)
        for lane, size in column_blocks(hidden)
    }
    for k in range(replicas):
        peer = replica ^ k
        at = 0
        for block in range(0, slots, LANES):
            for lane, size in column_blocks(hidden):
                packs[k][at : at + size, :] = turned[block, lane]
                at += size
        for lane in range(0, share, LANES):
            column = pl.multiple_of(width + peer * share + lane, LANES)
            packs[k][at : at + half, :] = x_ref[:, pl.ds(column, LANES)]
            packs[k][at + half : at + rows, :] = far_ref[:, pl.ds(column, LANES)]
            at += rows
        packs[k][at : at + half, :] = x_ref[:, 2 * width :]
        packs[k][at + half : at + rows, :] = far_ref[:, 2 * width :]
    for copy in downs:
        copy.wait()


def outputs_kernel(
    lead, activations, slope_ref, swish_ref, grads_ref, picker_ref, gain_ref, gate_w, up_w, unused, down_hbm,
    keep_ref, send_one, send_two, down_w, results, backs, turned, sems
):
    experts, _, width = gate_w.shape
    half = keep_ref.shape[0]
    slots = activations.shape[0]
    per_expert = slots // experts
    copies = fetch_experts((down_hbm,), (down_w,), sems, lead, experts)
    for copy in copies:
        copy.start()
    def arrive(e):
        if e >= lead and (e - lead) % 2 == 0:
            for copy in copies[e - lead : e - lead + 2]:
                copy.wait()

    def turn(e, part):
        if e < experts:
            turn_block(down_w.at[e], turned.at[e % TURNED], part, 4)

    def place(e):
        return slice(e * per_expert, (e + 1) * per_expert)

    arrive(0)
    for e in range(experts + 1):
        arrive(e + 1)
        turn(e + 1, 0)
        if e < experts:
            here = place(e)
            if e > 0:
                act_grad = jnp.dot(grads_ref[here, :], turned[e % TURNED], preferred_element_type=F32)
            else:
                act_grad = lax.dot_general(
                    grads_ref[here, :], down_w[e], NT, preferred_element_type=F32
                )
            backs[0, here, :] = (act_grad * slope_ref[here, :]).astype(BF16)
            backs[1, here, :] = (act_grad * swish_ref[here, :]).astype(BF16)
        turn(e + 1, 1)
        if e < experts:
            forward = jnp.dot(activations[here, :], down_w[e], preferred_element_type=F32)
            results[here, :width] = (
                forward.astype(BF16).astype(F32) * gain_ref[here, :]
            ).astype(BF16)
        turn(e + 1, 2)
        if e > 0:
            there = place(e - 1)
            back = jnp.dot(backs[0, there, :], gate_w[e - 1], preferred_element_type=F32)
        turn(e + 1, 3)
        if e > 0:
            back = back + jnp.dot(backs[1, there, :], up_w[e - 1], preferred_element_type=F32)
            results[there, width:] = back.astype(BF16)

    step = min(512, width)
    for at in range(0, 2 * width, step):
        total = jnp.dot(picker_ref[...], results[:, at : at + step], preferred_element_type=F32)
        keep_ref[:, at : at + step] = total[:half].astype(BF16)
        send_ref = send_one if at < width else send_two
        to = at % width
        send_ref[:, to : to + step] = total[half:].astype(BF16)


def grad_kernel(sizes, *refs):
    top, capacity, groups, tensor, replicas = sizes
    packs = refs[:replicas]
    own_ref, out_hbm, own_out, grads, acts, result, sems = refs[replicas:]
    experts, hidden, share = out_hbm.shape
    per_replica = groups * capacity
    slots = experts * per_replica
    per_expert = replicas * per_replica
    act_rows = slots // LANES * hidden
    rows = (packs[0].shape[0] - act_rows) // (share // LANES + 1)

    first_expert = (lax.axis_index("expert") * experts).astype(F32)
    token = row_tokens(rows, groups * tensor, tensor)
    for k in range(replicas):
        at = act_rows
        routing = packs[k][at + (share // LANES) * rows :, :].astype(F32)
        chosen, gains = slot_tables(
            routing, token, top, first_expert, capacity, groups, slots
        )
        scatter = chosen.T.astype(BF16)
        gain = jnp.sum(gains.T, axis=1, keepdims=True)
        for lane in range(0, share, LANES):
            filled = jnp.dot(scatter, packs[k][at : at + rows, :], preferred_element_type=F32)
            filled = (gain * filled).astype(BF16)
            for e in range(experts):
                to = e * per_expert + k * per_replica
                grads[to : to + per_replica, lane : lane + LANES] = filled[
                    e * per_replica : (e + 1) * per_replica
                ]
            at += rows

    left = jnp.concatenate(
        [
            packs[k][block * hidden : (block + 1) * hidden, :]
            for k in range(replicas)
            for block in range(slots // LANES)
        ],
        axis=1,
    )
    if experts > 1:
        lanes = replicas * slots
        before = fiota((lanes, lanes), 0)
        after = fiota((lanes, lanes), 1)
        source = whole_part(before, slots)
        inner = before - source * slots
        expert = whole_part(inner, per_replica)
        place = expert * per_expert + source * per_replica + inner - expert * per_replica
        order = jnp.where(place == after, 1.0, 0.0).astype(BF16)
        left = jnp.dot(left, order, preferred_element_type=F32).astype(BF16)
    acts[...] = left

    own_out[...] = own_ref[...].astype(F32)

    copies = []
    for e in range(experts):
        low = e * per_expert // LANES * LANES
        high = -(-(e + 1) * per_expert // LANES) * LANES
        right = grads[low:high, :]
        if high - low > per_expert:
            row = lax.broadcasted_iota(jnp.int32, right.shape, 0) + low
            inside = (row >= e * per_expert) & (row < (e + 1) * per_expert)
            right = jnp.where(inside, right.astype(F32), 0.0).astype(BF16)
        total = jnp.dot(acts[:, low:high], right, preferred_element_type=F32)
        result[e] = (total * (1.0 / replicas)).astype(BF16)
        copies.append(pltpu.make_async_copy(result.at[e], out_hbm.at[e], sems.at[e]))
        copies[-1].start()
    for copy in copies:
        copy.wait()


def near_kernel(mine, keep_ref, one_ref, two_ref, own_ref, *parts):
    width = one_ref.shape[1]
    for k, part in enumerate((own_ref, *parts)):
        here = slice(k * mine, (k + 1) * mine)
        for side, ref in enumerate((one_ref, two_ref)):
            columns = slice(side * width, (side + 1) * width)
            part[:, columns] = (
                keep_ref[here, columns].astype(F32) + ref[here, :].astype(F32)
            ).astype(part.dtype)


def hbm_specs(count):
    return [pl.BlockSpec(memory_space=pltpu.HBM)] * count


def vmem_specs(count):
    return [pl.BlockSpec(memory_space=pltpu.VMEM)] * count


def shards(
    tokens, routes, positions, combine_weights, cotangent, gate_weight, up_weight, down_weight
):
    experts, width, hidden = gate_weight.shape
    replicas = lax.axis_size("dp")
    groups = lax.axis_size("expert")
    tensor = lax.axis_size("tensor")
    group_size, top = routes.shape
    capacity = group_size // 2
    slots = experts * groups * capacity
    mine = tokens.shape[0]
    devices = groups * tensor
    rows = mine * devices
    both = ("expert", "tensor")

    def swap(values, distance):
        return lax.ppermute(values, both, [(i, i ^ distance) for i in range(devices)])

    weights = [
        pltpu.with_memory_space_constraint(jnp.swapaxes(w, 1, 2), pltpu.HBM)
        for w in (gate_weight, up_weight, down_weight)
    ]
    held = pltpu.VMEM((experts, hidden, width), BF16)
    ready = min(EARLY, experts)
    inputs = [
        pltpu.with_memory_space_constraint(x, pltpu.HBM)
        for x in (tokens, cotangent, routes.T, positions.T, combine_weights.T)
    ]
    row = jax.ShapeDtypeStruct((mine, 2 * width + LANES), BF16)
    sent = pl.pallas_call(
        pack_kernel,
        out_shape=row,
        in_specs=hbm_specs(5),
        out_specs=vmem_specs(1)[0],
        scratch_shapes=[
            pltpu.VMEM((mine, width), BF16),
            pltpu.VMEM((mine, width), BF16),
            pltpu.VMEM((top, group_size), jnp.int32),
            pltpu.VMEM((top, group_size), jnp.int32),
            pltpu.VMEM((top, group_size), F32),
            pltpu.SemaphoreType.DMA((5,)),
        ],
        compiler_params=pltpu.CompilerParams(vmem_limit_bytes=2 * 2**20),
        name="pack",
    )(*inputs)
    held_weights = pl.pallas_call(
        functools.partial(fetch_kernel, ready),
        out_shape=[held] * 2,
        in_specs=hbm_specs(2),
        out_specs=vmem_specs(2),
        scratch_shapes=[pltpu.SemaphoreType.DMA((experts, 2))],
        compiler_params=pltpu.CompilerParams(vmem_limit_bytes=2**20),
        name="fetch",
    )(*weights[:2])
    blocks = devices // 2
    kept = [pltpu.with_memory_space_constraint(w, pltpu.VMEM) for w in held_weights]
    near_rows, *held_weights = pl.pallas_call(
        join_kernel,
        out_shape=[jax.ShapeDtypeStruct((rows // 2, 2 * width + LANES), BF16)] + [held] * 2,
        in_specs=vmem_specs(blocks + 2),
        out_specs=vmem_specs(3),
        input_output_aliases={blocks: 1, blocks + 1: 2},
        compiler_params=pltpu.CompilerParams(vmem_limit_bytes=2 * 2**20),
        name="join",
    )(sent, *[swap(sent, 2 * k) for k in range(1, blocks)], *kept)
    far_rows = swap(near_rows, 1)

    pack_rows = slots // LANES * hidden + (width // replicas // LANES + 1) * rows
    half = jax.ShapeDtypeStruct((rows // 2, 2 * width), BF16)
    pack = jax.ShapeDtypeStruct((pack_rows, LANES), BF16)
    kept = [pltpu.with_memory_space_constraint(w, pltpu.VMEM) for w in held_weights]
    lead = min(LEAD, experts)
    slot_wide = jax.ShapeDtypeStruct((slots, width), BF16)
    slot_narrow = jax.ShapeDtypeStruct((slots, hidden), F32)
    outs = pl.pallas_call(
        functools.partial(
            activations_kernel, (top, capacity, groups, tensor, replicas), ready, lead
        ),
        out_shape=[held] * 3
        + [
            jax.ShapeDtypeStruct((slots, hidden), BF16),
            slot_narrow,
            slot_narrow,
            slot_wide,
            jax.ShapeDtypeStruct((rows, slots), BF16),
            jax.ShapeDtypeStruct((slots, 1), F32),
        ]
        + [pack] * replicas,
        in_specs=vmem_specs(2) + hbm_specs(3) + vmem_specs(2),
        out_specs=vmem_specs(9 + replicas),
        scratch_shapes=[
            pltpu.VMEM((slots, width), BF16),
            pltpu.SemaphoreType.DMA((experts, 2)),
            pltpu.SemaphoreType.DMA((experts, 1)),
        ],
        input_output_aliases={5: 0, 6: 1},
        compiler_params=pltpu.CompilerParams(vmem_limit_bytes=6 * 2**20),
        cost_estimate=pl.CostEstimate(
            flops=4 * slots * hidden * width,
            bytes_accessed=4 * experts * hidden * width,
            transcendentals=slots * hidden,
        ),
        name="activations",
    )(near_rows, far_rows, *weights, *kept)
    kept = [pltpu.with_memory_space_constraint(w, pltpu.VMEM) for w in outs[:3]]
    packs = outs[9:]
    side = jax.ShapeDtypeStruct((rows // 2, width), BF16)
    keep, send_one, send_two, _ = pl.pallas_call(
        functools.partial(outputs_kernel, lead),
        out_shape=[half, side, side, held],
        in_specs=vmem_specs(9) + hbm_specs(1),
        out_specs=vmem_specs(4),
        scratch_shapes=[
            pltpu.VMEM((slots, 2 * width), BF16),
            pltpu.VMEM((2, slots, hidden), BF16),
            pltpu.VMEM((TURNED, width, hidden), BF16),
            pltpu.SemaphoreType.DMA((experts, 1)),
        ],
        input_output_aliases={8: 3},
        compiler_params=pltpu.CompilerParams(vmem_limit_bytes=6 * 2**20),
        cost_estimate=pl.CostEstimate(
            flops=8 * slots * hidden * width,
            bytes_accessed=6 * experts * hidden * width,
            transcendentals=0,
        ),
        name="outputs",
    )(*outs[3:9], *kept, weights[2])

    own, *others_near = pl.pallas_call(
        functools.partial(near_kernel, mine),
        out_shape=[jax.ShapeDtypeStruct((mine, 2 * width), F32)]
        + [jax.ShapeDtypeStruct((mine, 2 * width), BF16)] * (devices // 2 - 1),
        in_specs=vmem_specs(3),
        out_specs=vmem_specs(devices // 2),
        compiler_params=pltpu.CompilerParams(vmem_limit_bytes=2 * 2**20),
        name="near",
    )(keep, swap(send_one, 1), swap(send_two, 1))
    received = [swap(part, 2 * k) for k, part in enumerate(others_near, 1)]

    arrived = [packs[0]]
    for k in [*range(2, replicas), 1]:
        arrived.append(lax.ppermute(packs[k], "dp", [(i, i ^ k) for i in range(replicas)]))
    share = width // replicas
    grad, total = pl.pallas_call(
        functools.partial(grad_kernel, (top, capacity, groups, tensor, replicas)),
        out_shape=[
            jax.ShapeDtypeStruct((experts, hidden, share), BF16),
            jax.ShapeDtypeStruct((mine, 2 * width), F32),
        ],
        in_specs=vmem_specs(replicas + 1),
        out_specs=[pl.BlockSpec(memory_space=pl.ANY)] + vmem_specs(1),
        scratch_shapes=[
            pltpu.VMEM((replicas * slots, share), BF16),
            pltpu.VMEM((hidden, replicas * slots), BF16),
            pltpu.VMEM((experts, hidden, share), BF16),
            pltpu.SemaphoreType.DMA((experts,)),
        ],
        compiler_params=pltpu.CompilerParams(vmem_limit_bytes=10 * 2**20),
        cost_estimate=pl.CostEstimate(
            flops=2 * replicas * slots * share * hidden,
            bytes_accessed=2 * experts * share * hidden,
            transcendentals=0,
        ),
        name="grad_down",
    )(*arrived, own)
    total = (total + sum(part.astype(F32) for part in received[-1:] + received[:-1])).astype(BF16)
    return (total[:, :width], total[:, width:], jnp.swapaxes(grad, 1, 2))


def solution(mesh):
    return jax.shard_map(
        shards,
        mesh=mesh,
        in_specs=(
            P(("dp", "expert", "tensor"), None),
            P(("dp", "expert"), None),
            P(("dp", "expert"), None),
            P(("dp", "expert"), None),
            P(("dp", "expert", "tensor"), None),
            P("expert", None, "tensor"),
            P("expert", None, "tensor"),
            P("expert", None, "tensor"),
        ),
        out_specs=(
            P(("dp", "expert", "tensor"), None),
            P(("dp", "expert", "tensor"), None),
            P("expert", "dp", "tensor"),
        ),
        check_vma=False,
    )
```
